32 devices in a mesh: modes: 4 (over y, core), space: 8 (over z, x).
Axes of the slice: x: 2, y: 2, z: 4, core: 2. Of those that a mesh axis runs over, the one named last changes fastest.
Arguments:
- thermal_deviation_iterate: float32 [4, 32, 256], P(None, 'space'), may hold values from -6 to 6
- volumetric_source_term: float32 [4, 32, 256], P(None, 'space'), may hold values from -6 to 6
- node_substance_label: int32 [4, 32, 256], P(None, 'space'), may hold values from 0 to 2
- spectral_table_lookup: int32 [40], P('modes'), may hold values from 0 to 63
- propagation_velocity_table: float32 [64], replicated, may hold values from 0.7 to 1
- specific_heat_table: float32 [64], replicated, may hold values from 0.5 to 2
- collision_frequency_table: float32 [64, 3], replicated, may hold values from 0.08 to 0.4
- ordinate_inclination: float32 [30], replicated, may hold values from 0.05 to 1.52
- ordinate_longitude: float32 [30], replicated, may hold values from -3.140625 to 3.140625
Outputs:
- new_temperature: float32 [4, 32, 256], P(None, 'space', 'modes')
- heat_flux: float32 [3, 4, 32, 256], P(None, None, 'space', 'modes')
The draws below stay inside these ranges and needn't reach their ends.
All inputs are finite; a program needn't handle non-finite values.
Results may differ from the reference program's by a relative error of at most 0.000078.
Values sent between devices are 32-bit elements; how exact they have to be, the bound alone decides.
No kernel may reach another device: no remote copies, remote signals or barrier semaphores. Data moves between devices by JAX's collectives and lax.ppermute only.
A program may use at most 64 MiB of HBM per device.

```python
import math
import jax
import jax.numpy as jnp
from jax import lax

SPECTRAL_BINS = 40
HALF_DIR = 30
ANGULAR_ORDINATES = 60
TABLE = 64
LATERAL_NODES_V = 256
SLAB_LAYERS = 4
SWEEPS = 3
CHEB = 16
LATERAL_NODES_U = 32


def with_ends(values, key, least, largest):
    shape = values.shape
    spot = [jax.random.randint(jax.random.fold_in(key, axis), (), 0, shape[axis]) for axis in range(len(shape))]
    values = values.at[tuple(spot)].set(least)
    longest = shape.index(max(shape))
    spot[longest] = (spot[longest] + 1) % shape[longest]
    return values.at[tuple(spot)].set(largest)


def steps_of(rng, extent, pieces, least, largest):
    loudness = 1.0
    for dim, parts in pieces:
        steps = jax.random.uniform(jax.random.fold_in(jax.random.fold_in(rng, 6), dim), (parts,), jnp.float32, least / len(pieces), largest / len(pieces))
        loudness = loudness * jnp.repeat(jnp.exp(steps), extent[dim] // parts).reshape((-1,) + (1,) * (len(extent) - 1 - dim))
    return loudness


def scatter_about(rng, shape, deviation, bound, split=(), held_as=jnp.bfloat16):
    gain = steps_of(rng, shape, split, -0.22, 0.18) if split else 1.0
    drawn = jax.random.normal(rng, shape, jnp.float32) * deviation * gain
    return jnp.minimum(jnp.maximum(drawn, -bound), bound).astype(held_as)


def setup_inputs(seed: int = 0) -> dict:
    streams_of = jax.random.split(jax.random.key(seed), 10)
    thermal_deviation_iterate = scatter_about(streams_of[0], (SLAB_LAYERS, LATERAL_NODES_U, LATERAL_NODES_V), 1.0, 6.0, ((1, 8),), jnp.float32)
    volumetric_source_term = scatter_about(streams_of[1], (SLAB_LAYERS, LATERAL_NODES_U, LATERAL_NODES_V), 1.0, 6.0, ((1, 8),), jnp.float32)
    node_substance_label = with_ends(jax.random.randint(streams_of[2], (SLAB_LAYERS, LATERAL_NODES_U, LATERAL_NODES_V), 0, 3), jax.random.fold_in(streams_of[2], 1), 0, 2).astype(jnp.int32)
    spectral_table_lookup = with_ends(jax.random.randint(streams_of[3], (SPECTRAL_BINS,), 0, TABLE), jax.random.fold_in(streams_of[3], 1), 0, TABLE - 1).astype(jnp.int32)
    propagation_velocity_table = jnp.clip(jax.random.uniform(streams_of[4], (TABLE,), jnp.float32, 0.7, 1.0), 0.7, 1.0)
    specific_heat_table = jnp.clip(jnp.exp(jax.random.uniform(streams_of[5], (TABLE,), jnp.float32, math.log(0.5), math.log(2.0))), 0.5, 2.0)
    collision_frequency_table = jnp.clip(jnp.exp(jax.random.uniform(streams_of[6], (TABLE, 3), jnp.float32, math.log(0.08), math.log(0.4))), 0.08, 0.4)
    ordinate_inclination = jnp.clip(jax.random.uniform(streams_of[7], (HALF_DIR,), jnp.float32, 0.05, 1.52), 0.05, 1.52)
    ordinate_longitude = jnp.clip(jax.random.uniform(streams_of[8], (HALF_DIR,), jnp.float32, -3.140625, 3.140625), -3.140625, 3.140625)
    return dict(thermal_deviation_iterate=thermal_deviation_iterate, volumetric_source_term=volumetric_source_term, node_substance_label=node_substance_label, spectral_table_lookup=spectral_table_lookup, propagation_velocity_table=propagation_velocity_table, specific_heat_table=specific_heat_table, collision_frequency_table=collision_frequency_table, ordinate_inclination=ordinate_inclination, ordinate_longitude=ordinate_longitude)


def directions(ordinate_inclination, ordinate_longitude):
    along_x = jnp.cos(ordinate_inclination)
    along_y = jnp.sin(ordinate_inclination) * jnp.cos(ordinate_longitude)
    along_z = jnp.sin(ordinate_inclination) * jnp.sin(ordinate_longitude)
    return (jnp.concatenate([along_x, -along_x]), jnp.concatenate([along_y, -along_y]),
            jnp.concatenate([along_z, -along_z]))


def diffuse_apply(padded_values, padded_kappa):
    center = padded_values[1:-1, 1:-1, 1:-1]
    kappa_here = padded_kappa[1:-1, 1:-1, 1:-1]
    slices = [(slice(1, -1), slice(None, -2), slice(1, -1)), (slice(1, -1), slice(2, None), slice(1, -1)),
              (slice(1, -1), slice(1, -1), slice(None, -2)), (slice(1, -1), slice(1, -1), slice(2, None)),
              (slice(None, -2), slice(1, -1), slice(1, -1)), (slice(2, None), slice(1, -1), slice(1, -1))]
    total = jnp.zeros_like(center)
    for where in slices:
        total = total + 0.5 * (kappa_here + padded_kappa[where]) * (center - padded_values[where])
    return center + total


def reference(thermal_deviation_iterate, volumetric_source_term, node_substance_label, spectral_table_lookup, propagation_velocity_table, specific_heat_table, collision_frequency_table, ordinate_inclination, ordinate_longitude):
    velocity = propagation_velocity_table[spectral_table_lookup]
    spectral = (jnp.arange(SPECTRAL_BINS).astype(jnp.float32) + 1.0) / SPECTRAL_BINS
    specific_thermal_storage = specific_heat_table[spectral_table_lookup] * spectral
    rates = collision_frequency_table[spectral_table_lookup]
    along_x, along_y, along_z = directions(ordinate_inclination, ordinate_longitude)
    masks = [(node_substance_label == kind).astype(jnp.float32) for kind in range(3)]
    node_collision_frequency = (rates[:, 0, None, None, None] * masks[0] + rates[:, 1, None, None, None] * masks[1]
                 + rates[:, 2, None, None, None] * masks[2])[:, None]
    speed_x = velocity[:, None] * along_x[None, :]
    speed_y = velocity[:, None] * along_y[None, :]
    speed_z = velocity[:, None] * along_z[None, :]

    def expand(coef):
        return coef[:, :, None, None, None]

    abs_sum = jnp.abs(along_x) + jnp.abs(along_y) + jnp.abs(along_z)
    denom = expand(velocity[:, None] * abs_sum[None, :]) + node_collision_frequency
    equilibrium_emission = specific_thermal_storage[:, None, None, None, None] * (node_collision_frequency * thermal_deviation_iterate + volumetric_source_term)
    iteration_bundle = jnp.broadcast_to(specific_thermal_storage[:, None, None, None, None] * thermal_deviation_iterate, (SPECTRAL_BINS, ANGULAR_ORDINATES) + thermal_deviation_iterate.shape)
    for sweep_index in range(SWEEPS):
        xpad = jnp.pad(iteration_bundle, ((0, 0), (0, 0), (0, 0), (1, 1), (0, 0)))
        ypad = jnp.pad(iteration_bundle, ((0, 0), (0, 0), (0, 0), (0, 0), (1, 1)))
        zpad = jnp.pad(iteration_bundle, ((0, 0), (0, 0), (1, 1), (0, 0), (0, 0)))
        xterm = expand(jnp.maximum(speed_x, 0.0)) * xpad[:, :, :, :-2] + expand(jnp.maximum(-speed_x, 0.0)) * xpad[:, :, :, 2:]
        yterm = expand(jnp.maximum(speed_y, 0.0)) * ypad[..., :-2] + expand(jnp.maximum(-speed_y, 0.0)) * ypad[..., 2:]
        zterm = expand(jnp.maximum(speed_z, 0.0)) * zpad[:, :, :-2] + expand(jnp.maximum(-speed_z, 0.0)) * zpad[:, :, 2:]
        iteration_bundle = (xterm + yterm + zterm + equilibrium_emission) / denom
    summed = jnp.sum(iteration_bundle, axis=1)
    numer = jnp.sum(node_collision_frequency[:, 0] * summed, axis=0) / ANGULAR_ORDINATES
    fluxes = [jnp.einsum('fd,fdpxy->pxy', coef, iteration_bundle, precision=lax.Precision.HIGHEST) / ANGULAR_ORDINATES
              for coef in (speed_x, speed_y, speed_z)]
    rate_total = jnp.sum(specific_thermal_storage[:, None] * rates, axis=0)
    cond_total = jnp.sum((specific_thermal_storage * velocity * velocity)[:, None] / (3.0 * rates), axis=0)
    conduct = cond_total / rate_total
    kappa = conduct[0] * masks[0] + conduct[1] * masks[1] + conduct[2] * masks[2]
    cell_total = rate_total[0] * masks[0] + rate_total[1] * masks[1] + rate_total[2] * masks[2]
    hemisphere_ordinates = numer / cell_total
    top = 1.0 + 12.0 * jnp.max(conduct)
    theta = (top + 1.0) / 2.0
    delta = (top - 1.0) / 2.0
    sigma = theta / delta
    padded_kappa = jnp.pad(kappa, 1)
    correction = jnp.zeros_like(hemisphere_ordinates)
    equation_mismatch = hemisphere_ordinates - thermal_deviation_iterate
    direction = equation_mismatch / theta
    rho = 1.0 / sigma
    for cheb_index in range(CHEB):
        correction = correction + direction
        equation_mismatch = equation_mismatch - diffuse_apply(jnp.pad(direction, 1), padded_kappa)
        rho_new = 1.0 / (2.0 * sigma - rho)
        direction = (rho_new * rho) * direction + (2.0 * rho_new / delta) * equation_mismatch
        rho = rho_new
    return hemisphere_ordinates + correction, jnp.stack(fluxes)
```

```python
import itertools

import jax
import jax.numpy as jnp
from jax import lax
from jax.experimental import pallas as pl
from jax.experimental.pallas import tpu as pltpu
from jax.sharding import PartitionSpec as P


SWEEPS = 3
CHEB = 16
PART = 32
CODES = (0, 1, 6)
HIGHEST = lax.Precision.HIGHEST


def monomials(degree):
    found = []
    for axes in itertools.combinations_with_replacement(range(3), degree):
        distinct = sorted(set(axes))
        for rest in itertools.product((-1, 1), repeat=max(len(distinct) - 1, 0)):
            found.append((axes, tuple(zip(distinct, (-1,) + rest)) if distinct else ()))
    return found


MONO = {degree: monomials(degree) for degree in range(4)}


def canonical(steps):
    axes = tuple(sorted(axis for axis, _ in steps))
    signs = dict(steps)
    first = signs[axes[0]]
    pattern = tuple((axis, signs[axis] * -first) for axis in sorted(signs))
    return (axes, pattern), -first


PAIRS = {(CODES[a] + CODES[b]) & 7: (a, b) for a, b in itertools.combinations_with_replacement(range(3), 2)}
TRIPLES = {
    CODES[a] + CODES[b] + CODES[c]: (a, b, c) for a, b, c in itertools.combinations_with_replacement(range(3), 3)
}
SINGLES = {CODES[a]: (a,) for a in range(3)}
LOW = {code: labels for code, labels in TRIPLES.items() if code < 8}
HIGH = {code & 7: labels for code, labels in TRIPLES.items() if code >= 8}
GROUPS = {
    "u3": (3, False, PAIRS),
    "u2": (2, False, PAIRS),
    "u1d": (2, False, SINGLES),
    "u1": (1, False, SINGLES),
    "u0d": (1, True, SINGLES),
    "u0": (0, True, SINGLES),
    "a3": (4, False, LOW),
    "b3": (4, False, HIGH),
    "a2": (3, False, LOW),
    "b2": (3, False, HIGH),
    "v1d": (3, False, PAIRS),
    "v1": (2, False, PAIRS),
    "f0d": (2, False, SINGLES),
}
GROUP_AT = {name: at for at, name in enumerate(GROUPS)}
COLUMNS = (
    [("u", degree, mono) for degree in (3, 2, 1, 0) for mono in MONO[degree]]
    + [("v", degree, mono) for degree in (3, 2, 1) for mono in MONO[degree]]
    + [(axis, degree, mono) for axis in range(3) for degree in (3, 2, 1) for mono in MONO[degree]]
)
COLUMN_AT = {column: at for at, column in enumerate(COLUMNS)}
COLUMN_TILES = -(-len(COLUMNS) // 128)


def table_list():
    found = [("inverse_rate",), ("conduct",), ("inverse_theta",)]
    found += [("keep", step) for step in range(CHEB - 1)] + [("gain", step) for step in range(CHEB - 1)]
    for group, degree in (("u3", 3), ("u2", 2), ("u1d", 2), ("u1", 1), ("u0d", 1), ("u0", 0)):
        found += [(group, "u", degree, mono) for mono in MONO[degree]]
    for kind in ("v", 0, 1, 2):
        for group, degree in (("a3", 3), ("b3", 3), ("a2", 2), ("b2", 2), ("v1d", 2), ("v1", 1)):
            found += [(group, kind, degree, mono) for mono in MONO[degree]]
    for kind in (0, 1, 2):
        found += [("f0d", kind, 1, mono) for mono in MONO[1]]
    return found


TABLES = table_list()
TABLE_AT = {key: at for at, key in enumerate(TABLES)}


def lanes(shape):
    return lax.broadcasted_iota(jnp.int32, shape, len(shape) - 1)


def sublanes(shape):
    return lax.broadcasted_iota(jnp.int32, shape, len(shape) - 2)


def pack_kernel(lookup_ref, values_ref, source_ref, label_ref, out_ref):
    planes, rows, _ = values_ref.shape
    part = rows * planes // 8
    for plane in range(planes):
        for row in range(rows):
            at, sub = divmod(row * planes + plane, 8)
            out_ref[at, sub : sub + 1, :] = values_ref[plane, row : row + 1, :]
            out_ref[part + at, sub : sub + 1, :] = source_ref[plane, row : row + 1, :]
            out_ref[2 * part + at, sub : sub + 1, :] = (label_ref[plane, row : row + 1, :] + 1).astype(jnp.float32)
    lane = lanes(out_ref.shape[1:])
    first = lax.axis_index("modes") * PART
    found = jnp.zeros(out_ref.shape[1:], jnp.int32)
    for at in range(lookup_ref.shape[0]):
        found = jnp.where(lane == first + at, lookup_ref[at] + 1, found)
    out_ref[3 * part] = found.astype(jnp.float32)


def table_kernel(parts, per_part, *refs):
    lookups = refs[: -8]
    velocity_ref, heat_ref, rate_ref, polar_ref, azimuth_ref, out_ref, work_ref, axes_ref = refs[-8:]
    half_dir = polar_ref.shape[0]
    size = velocity_ref.shape[0]
    padded = -(-per_part // 8) * 8
    lane = lanes((1, 128))

    found = lookups[0][0, 0:1, 0:128]
    for ref in lookups[1:]:
        found = found + ref[0, 0:1, 0:128]
    index = found.astype(jnp.int32) - 1
    valid = index >= 0
    work_ref[0:8, :] = jnp.zeros((8, 128), jnp.float32)
    work_ref[0, 0:size] = velocity_ref[...]
    work_ref[1, 0:size] = heat_ref[...]
    work_ref[2:5, 0:size] = rate_ref[...]
    table = work_ref[0:8, :]
    index = jnp.broadcast_to(jnp.where(valid, index, 0), (8, 128))
    picked = jnp.take_along_axis(table, index, axis=1, mode="promise_in_bounds")
    frequency = (lane // PART) * per_part + lane % PART
    spectral = (frequency.astype(jnp.float32) + 1.0) / (parts * per_part)
    velocity = jnp.where(valid, picked[0:1], 1.0)
    capacity = jnp.where(valid, picked[1:2] * spectral, 0.0)
    rates = [jnp.where(valid, picked[2 + k : 3 + k], 1.0) for k in range(3)]

    conducts, inverses = [], []
    for k in range(3):
        rate_total = jnp.sum(capacity * rates[k], axis=1, keepdims=True)
        cond_total = jnp.sum(capacity * velocity * velocity / (3.0 * rates[k]), axis=1, keepdims=True)
        conducts.append(cond_total / rate_total)
        inverses.append(1.0 / (2 * half_dir * rate_total))
    sub = sublanes((8, 128))

    def by_label(values):
        found = jnp.zeros((8, 128), jnp.float32)
        for code, value in zip(CODES, values):
            found = jnp.where(sub == code, value, found)
        return found

    out_ref[TABLE_AT["inverse_rate",]] = by_label(inverses)
    out_ref[TABLE_AT["conduct",]] = by_label(conducts)
    top = 1.0 + 12.0 * jnp.maximum(jnp.maximum(conducts[0], conducts[1]), conducts[2])
    top = jnp.broadcast_to(top, (8, 128))
    theta = (top + 1.0) / 2.0
    delta = (top - 1.0) / 2.0
    sigma = theta / delta
    rho = 1.0 / sigma
    out_ref[TABLE_AT["inverse_theta",]] = 1.0 / theta
    for step in range(CHEB - 1):
        rho_new = 1.0 / (2.0 * sigma - rho)
        out_ref[TABLE_AT["keep", step]] = rho_new * rho
        out_ref[TABLE_AT["gain", step]] = 2.0 * rho_new / delta
        rho = rho_new

    axes_ref[0:8, :] = jnp.zeros((8, 128), jnp.float32)
    for part in range(parts):
        axes_ref[0, part * PART : part * PART + half_dir] = polar_ref[...]
        axes_ref[1, part * PART : part * PART + half_dir] = azimuth_ref[...]
    angles = axes_ref[0:8, :]
    cosines, sines = jnp.cos(angles), jnp.sin(angles)
    real = (lane % PART) < half_dir
    u = [cosines[0:1], sines[0:1] * cosines[1:2], sines[0:1] * sines[1:2]]
    u = [jnp.where(real, part, 0.0) for part in u]
    a = [jnp.abs(part) for part in u]
    total = a[0] + a[1] + a[2]
    sides = [jnp.where(part >= 0.0, 1.0, -1.0) for part in u]

    products = {(): jnp.where(real, 1.0, 0.0)}
    for degree in (1, 2, 3):
        for axes in itertools.combinations_with_replacement(range(3), degree):
            products[axes] = products[axes[:-1]] * a[axes[-1]]
    masks = {}
    for degree in range(4):
        for _, pattern in MONO[degree]:
            if pattern not in masks:
                same = flipped = jnp.ones((1, 128), jnp.float32)
                for axis, sign in pattern:
                    if axis == 0:
                        flipped = jnp.zeros((1, 128), jnp.float32)
                    else:
                        same = same * jnp.where(sides[axis] == -sign, 1.0, 0.0)
                        flipped = flipped * jnp.where(sides[axis] == sign, 1.0, 0.0)
                masks[pattern] = (same + flipped, same - flipped)
    axes_ref[...] = jnp.zeros(axes_ref.shape, jnp.float32)
    weights = {"u": None, "v": total}
    weights.update({axis: u[axis] * (1.0 / (2 * half_dir)) for axis in range(3)})
    for at, (kind, degree, (axes, pattern)) in enumerate(COLUMNS):
        even, odd = masks[pattern]
        row = products[axes] * (even if kind in ("u", "v") else odd)
        if weights[kind] is not None:
            row = row * weights[kind]
        axes_ref[at : at + 1, :] = row

    columns = jnp.concatenate([velocity, capacity] + rates + [jnp.zeros((3, 128), jnp.float32)], axis=0).T

    def spread(at):
        found = jnp.zeros((padded, 128), jnp.float32)
        where = lanes((padded, 128)) // PART
        for part in range(parts):
            column = columns[part * PART : part * PART + padded, at : at + 1]
            found = jnp.where(where == part, column, found)
        return found

    speed, stored = spread(0), spread(1)
    loss = [spread(2 + k) for k in range(3)]
    inverse = [1.0 / (speed * total + loss[k]) for k in range(3)]
    weight = [stored]
    for _ in range(4):
        weight.append(weight[-1] * speed)
    chains = {}
    for length in (1, 2, 3):
        for labels in itertools.combinations_with_replacement(range(3), length):
            chains[labels] = inverse[labels[0]] if length == 1 else chains[labels[:-1]] * inverse[labels[-1]]
    work_ref[...] = jnp.zeros(work_ref.shape, jnp.float32)
    for name, (power, rated, index) in GROUPS.items():
        for code, labels in index.items():
            field = weight[power] * chains[labels]
            if rated:
                field = field * loss[labels[0]]
            at = GROUP_AT[name] * 8 + code
            work_ref[at : at + 1, :] = jnp.sum(field, axis=0, keepdims=True)
    sums = lax.dot_general(
        work_ref[...],
        axes_ref[...],
        (((1,), (1,)), ((), ())),
        precision=HIGHEST,
        preferred_element_type=jnp.float32,
    )
    for at, key in enumerate(TABLES):
        if len(key) == 4:
            row, column = GROUP_AT[key[0]] * 8, COLUMN_AT[key[1:]]
            out_ref[at] = jnp.broadcast_to(sums[row : row + 8, column : column + 1], (8, 128))


SIGNED = [(axis, sign) for axis in range(3) for sign in (-1, 1)]


def follows(earlier, step):
    return all((step[0], -step[1]) != before for before in earlier)


def displacement(steps):
    found = [0, 0, 0]
    for axis, sign in steps:
        found[axis] += sign
    return tuple(found)


def ends_of_two():
    found = {}
    for first in SIGNED:
        for second in SIGNED:
            if follows((first,), second):
                found.setdefault(tuple(sorted((first, second))), []).append(first)
    return found


ENDS = ends_of_two()
REACH = SWEEPS
FAR = [(z, y) for z in range(-3, 4) for y in range(-3, 4) if abs(z) + abs(y) <= 3]
NEAR = [(z, y) for z in range(-2, 3) for y in range(-2, 3) if abs(z) + abs(y) <= 2]
FAR_AT = {key: at for at, key in enumerate(FAR)}
NEAR_AT = {key: at for at, key in enumerate(NEAR)}


def pick(table, index):
    return jnp.take_along_axis(table, index, axis=0, mode="promise_in_bounds")


class Cells:
    def __init__(self, entry, far_ref, source_ref, code_ref):
        self.entry = entry
        self.refs = (far_ref, source_ref, code_ref)
        self.known = {}

    def get(self, which, place):
        key = (which, place)
        if key not in self.known:
            x, y, z = place
            at = FAR_AT[z, y] if which == 0 else NEAR_AT[z, y]
            self.known[key] = self.refs[which][at, self.entry + REACH + x]
        return self.known[key]

    def rise(self, place, step):
        further = list(place)
        further[step[0]] += step[1]
        return self.get(0, tuple(further)) - self.get(0, place)


class Sums:
    def __init__(self, count=4):
        self.parts = [None] * count
        self.at = 0

    def add(self, value):
        held = self.parts[self.at]
        self.parts[self.at] = value if held is None else held + value
        self.at = (self.at + 1) % len(self.parts)

    def total(self):
        held = [part for part in self.parts if part is not None]
        while len(held) > 1:
            held = [sum(held[at + 1 : at + 2], held[at]) for at in range(0, len(held), 2)]
        return held[0]


def energy_of(cells_list, table):
    sums = [Sums() for _ in cells_list]
    here = (0, 0, 0)
    codes = [cells.get(2, here) for cells in cells_list]
    rest = table(("u0", "u", 0, MONO[0][0]))
    for cells, code, held in zip(cells_list, codes, sums):
        held.add(pick(rest, code) * cells.get(1, here))
    for step in SIGNED:
        mono, _ = canonical((step,))
        rest = table(("u0d", "u", 1, mono))
        for cells, code, held in zip(cells_list, codes, sums):
            held.add(pick(rest, code) * cells.rise(here, step))
    two = {}
    for first in SIGNED:
        place = displacement((first,))
        mono, _ = canonical((first,))
        nears = [cells.get(2, place) for cells in cells_list]
        two[first] = [near + code for near, code in zip(nears, codes)]
        pairs = [both & 7 for both in two[first]]
        one, other = table(("u1", "u", 1, mono)), table(("v1", "v", 1, mono))
        for cells, near, pair, held in zip(cells_list, nears, pairs, sums):
            held.add((pick(one, near) - pick(other, pair)) * cells.get(1, place))
        for step in SIGNED:
            if follows((first,), step):
                mono, _ = canonical((first, step))
                one, other = table(("u1d", "u", 2, mono)), table(("v1d", "v", 2, mono))
                for cells, near, pair, held in zip(cells_list, nears, pairs, sums):
                    held.add((pick(one, near) - pick(other, pair)) * cells.rise(place, step))
    for steps, firsts in ENDS.items():
        place = displacement(steps)
        index = []
        for at, cells in enumerate(cells_list):
            end = cells.get(2, place)
            mine = []
            for first in firsts:
                near = cells.get(2, displacement((first,)))
                triple = two[first][at] + end
                mine.append(((near + end) & 7, triple & 7, triple >= 8))
            index.append(mine)
        cases = [(None, "2", canonical(steps)[0], 2)]
        cases += [(step, "3", canonical(steps + (step,))[0], 3) for step in SIGNED if follows(steps, step)]
        for step, which, mono, degree in cases:
            one = table(("u" + which, "u", degree, mono))
            low, high = table(("a" + which, "v", degree, mono)), table(("b" + which, "v", degree, mono))
            for cells, mine, held in zip(cells_list, index, sums):
                factor = None
                for pair, triple, above in mine:
                    term = pick(one, pair) - jnp.where(above, pick(high, triple), pick(low, triple))
                    factor = term if factor is None else factor + term
                held.add(factor * (cells.get(1, place) if step is None else cells.rise(place, step)))
    return [held.total() for held in sums]


def flux_of(cells, table):
    sums = [Sums(2) for _ in range(3)]
    here = (0, 0, 0)
    code = cells.get(2, here)

    def signed(value, side):
        return value if side > 0 else -value

    for step in SIGNED:
        mono, side = canonical((step,))
        rise = signed(cells.rise(here, step), side)
        for axis in range(3):
            sums[axis].add(pick(table(("f0d", axis, 1, mono)), code) * rise)
    two = {}
    for first in SIGNED:
        place = displacement((first,))
        two[first] = cells.get(2, place) + code
        pair = two[first] & 7
        mono, side = canonical((first,))
        value = signed(cells.get(1, place), side)
        for axis in range(3):
            sums[axis].add(pick(table(("v1", axis, 1, mono)), pair) * value)
        for step in SIGNED:
            if follows((first,), step):
                mono, side = canonical((first, step))
                value = signed(cells.rise(place, step), side)
                for axis in range(3):
                    sums[axis].add(pick(table(("v1d", axis, 2, mono)), pair) * value)
    for steps, firsts in ENDS.items():
        place = displacement(steps)
        end = cells.get(2, place)
        index = []
        for first in firsts:
            triple = two[first] + end
            index.append((triple & 7, triple >= 8))
        cases = [(None, "2", canonical(steps), 2)]
        cases += [(step, "3", canonical(steps + (step,)), 3) for step in SIGNED if follows(steps, step)]
        for step, which, (mono, side), degree in cases:
            value = signed(cells.get(1, place) if step is None else cells.rise(place, step), side)
            for axis in range(3):
                low, high = table(("a" + which, axis, degree, mono)), table(("b" + which, axis, degree, mono))
                factor = None
                for triple, above in index:
                    term = jnp.where(above, pick(high, triple), pick(low, triple))
                    factor = term if factor is None else factor + term
                sums[axis].add(factor * value)
    return [held.total() for held in sums]


def main_kernel(groups, places, *refs):
    blocks = refs[: 2 * groups]
    table_ref, temperature_ref, flux_ref, base_ref, source_base_ref, code_base_ref = refs[2 * groups : 2 * groups + 6]
    far_ref, near_ref, code_ref, kappa_ref, force_ref, half_ref, coef_ref, mismatch_ref, way_ref = refs[
        2 * groups + 6 :
    ]
    planes, rows, tile = temperature_ref.shape
    width = blocks[0].shape[2]
    parts = rows * planes // 8
    length = groups * rows
    lane, sub = lanes((8, 128)), sublanes((8, 128))
    lower = sub < planes
    plane = sub % planes
    modes = lax.axis_index("modes")
    leads, swaps, own_lead, own_upper = places()

    margin = (128 - tile) // 2
    start = modes * tile - margin
    column = start + lane
    inside = (column >= 0) & (column < width)
    tiles = width // 128
    left = (start + 128) // 128 - 1
    turn = 128 - (start - left * 128)
    from_left = lane < turn

    def window(wide):
        first, second = wide[:, 0:128], wide[:, 128:256]
        even = lax.rem(left + 2, 2) == 0
        one, two = jnp.where(even, first, second), jnp.where(even, second, first)
        return jnp.where(from_left, pltpu.roll(one, turn, axis=1), pltpu.roll(two, turn, axis=1))

    for group in range(groups):
        one, two = blocks[2 * group], blocks[2 * group + 1]
        swap = swaps[group]
        for which, ref in enumerate((base_ref, source_base_ref, code_base_ref)):
            for part in range(parts):
                first, second = one[which * parts + part], two[which * parts + part]
                low, high = jnp.where(swap, second, first), jnp.where(swap, first, second)
                low, high = window(low), window(high)
                pair = (
                    jnp.where(lower, low, pltpu.roll(high, planes, axis=0)),
                    jnp.where(lower, pltpu.roll(low, planes, axis=0), high),
                )
                for row in range(2):
                    at = REACH + leads[group] + 2 * part + row
                    if which < 2:
                        ref[at] = jnp.where(inside, pair[row], 0.0)
                    else:
                        ref[at] = jnp.where(inside, pair[row], 0.0).astype(jnp.int32)

    for ref in (base_ref, source_base_ref, code_base_ref):
        none = jnp.zeros((8, 128), ref.dtype)
        for at in range(REACH):
            ref[at] = jnp.where(lower, none, pltpu.roll(ref[at + length], planes, axis=0))
            ref[length + REACH + at] = jnp.where(lower, pltpu.roll(ref[REACH + at], planes, axis=0), none)

    conduct = table_ref[TABLE_AT["conduct",]]

    def shift_plane(value, z, none):
        if z == 0:
            return value
        return jnp.where((plane + z >= 0) & (plane + z < planes), pltpu.roll(value, (-z) % 8, axis=0), none)

    def shifted(at, _):
        for ref, out, keys in ((base_ref, far_ref, FAR_AT), (source_base_ref, near_ref, NEAR_AT)):
            value = ref[at]
            for y in sorted({y for _, y in keys}):
                moved = pltpu.roll(value, (-y) % 128, axis=1) if y else value
                for z in sorted({z for z, other in keys if other == y}):
                    out[keys[z, y], at] = shift_plane(moved, z, 0.0)
        label = code_base_ref[at]
        kind = jnp.maximum(label - 1, 0)
        code = jnp.where(kind == 2, CODES[2], kind)
        kappa_ref[at] = jnp.where(label > 0, pick(conduct, code), 0.0)
        for y in sorted({y for _, y in NEAR}):
            moved = pltpu.roll(code, (-y) % 128, axis=1) if y else code
            for z in sorted({z for z, other in NEAR if other == y}):
                code_ref[NEAR_AT[z, y], at] = pltpu.roll(moved, (-z) % 8, axis=0) if z else moved
        return 0

    lax.fori_loop(0, length + 2 * REACH, shifted, 0)

    def table(key):
        return table_ref[TABLE_AT[key]]

    def forcing(step, _):
        entries = (2 * step, 2 * step + 1)
        cells_list = [Cells(entry, far_ref, near_ref, code_ref) for entry in entries]
        energies = energy_of(cells_list, table)
        scale = table_ref[TABLE_AT["inverse_rate",]]
        for entry, cells, energy in zip(entries, cells_list, energies):
            force = energy * pick(scale, cells.get(2, (0, 0, 0)))
            force_ref[entry] = jnp.where(code_base_ref[entry + REACH] > 0, force, 0.0)
        return 0

    lax.fori_loop(0, length // 2, forcing, 0)

    none = jnp.zeros((8, 128), jnp.float32)
    inverse_theta = table_ref[TABLE_AT["inverse_theta",]]
    for entry in range(length):
        kappa = kappa_ref[entry + REACH]
        real = code_base_ref[entry + REACH] > 0
        others = [
            kappa_ref[entry + REACH - 1],
            kappa_ref[entry + REACH + 1],
            pltpu.roll(kappa, 1, axis=1),
            pltpu.roll(kappa, 127, axis=1),
            shift_plane(kappa, -1, 0.0),
            shift_plane(kappa, 1, 0.0),
        ]
        faces = [jnp.where(real, 0.5 * (kappa + other), 0.0) for other in others]
        coef_ref[6, entry] = 1.0 + ((faces[0] + faces[1]) + (faces[2] + faces[3]) + (faces[4] + faces[5]))
        faces[4] = jnp.where(plane >= 1, faces[4], 0.0)
        faces[5] = jnp.where(plane < planes - 1, faces[5], 0.0)
        for at in range(6):
            coef_ref[at, entry] = faces[at]
        mismatch_ref[entry] = force_ref[entry]
        way_ref[0, entry + 1] = force_ref[entry] * inverse_theta

    def edges(slot):
        way_ref[slot, 0] = jnp.where(lower, none, pltpu.roll(way_ref[slot, length], planes, axis=0))
        way_ref[slot, length + 1] = jnp.where(lower, pltpu.roll(way_ref[slot, 1], planes, axis=0), none)

    edges(0)
    for row in range(rows):
        half_ref[row] = way_ref[0, own_lead + row + 1]

    def advance(step, _):
        slot = lax.rem(step, 2)
        keep = table_ref[TABLE_AT["keep", 0] + step]
        gain = table_ref[TABLE_AT["gain", 0] + step]
        for entry in range(length):
            value = way_ref[slot, entry + 1]
            flow = coef_ref[6, entry] * value - coef_ref[0, entry] * way_ref[slot, entry]
            flow = flow - coef_ref[1, entry] * way_ref[slot, entry + 2]
            side = coef_ref[2, entry] * pltpu.roll(value, 1, axis=1)
            side = side + coef_ref[3, entry] * pltpu.roll(value, 127, axis=1)
            deep = coef_ref[4, entry] * pltpu.roll(value, 1, axis=0)
            deep = deep + coef_ref[5, entry] * pltpu.roll(value, 7, axis=0)
            mismatch = mismatch_ref[entry] - (flow - (side + deep))
            mismatch_ref[entry] = mismatch
            way_ref[1 - slot, entry + 1] = keep * value + gain * mismatch
        edges(1 - slot)
        for row in range(rows):
            half_ref[row] = half_ref[row] + way_ref[1 - slot, own_lead + row + 1]
        return 0

    lax.fori_loop(0, CHEB - 1, advance, 0)

    def cut(value):
        value = jnp.where(own_upper, pltpu.roll(value, planes, axis=0), value)
        return pltpu.roll(value, 128 - margin, axis=1)[0:planes, 0:tile]

    for row in range(rows):
        entry = own_lead + row
        found = cut(base_ref[entry + REACH] + force_ref[entry] + half_ref[row])
        for at in range(planes):
            temperature_ref[at, row : row + 1, :] = found[at : at + 1]

    def fluxes(row, _):
        cells = Cells(own_lead + row, far_ref, near_ref, code_ref)
        for axis, found in enumerate(flux_of(cells, table)):
            coef_ref[axis, row] = found
        return 0

    lax.fori_loop(0, rows, fluxes, 0)
    for axis in range(3):
        for row in range(rows):
            found = cut(coef_ref[axis, row])
            for at in range(planes):
                flux_ref[axis, at, row : row + 1, :] = found[at : at + 1]


def on_device(
    thermal_deviation_iterate,
    volumetric_source_term,
    node_substance_label,
    spectral_table_lookup,
    propagation_velocity_table,
    specific_heat_table,
    collision_frequency_table,
    ordinate_inclination,
    ordinate_longitude,
):
    planes, rows, width = thermal_deviation_iterate.shape
    modes, space = lax.axis_size("modes"), lax.axis_size("space")
    tile = width // modes
    per_part = spectral_table_lookup.shape[0]
    half_dir = ordinate_inclination.shape[0]
    assert planes * 2 == 8 and rows % 2 == 0 and width == 256
    assert modes * PART <= 128 and per_part <= PART and half_dir <= PART
    halo = -(-(CHEB - 1 + SWEEPS) // rows)
    reach = CHEB - 1 + SWEEPS
    assert tile + 2 * reach <= 128
    vmem = pl.BlockSpec(memory_space=pltpu.VMEM)
    smem = pl.BlockSpec(memory_space=pltpu.SMEM)
    parts = rows * planes // 8
    depth = 3 * parts + 1
    payload = pl.pallas_call(
        pack_kernel,
        out_shape=jax.ShapeDtypeStruct((depth, 8, width), jnp.float32),
        in_specs=[smem, vmem, vmem, vmem],
        out_specs=vmem,
        name="pack",
    )(spectral_table_lookup, thermal_deviation_iterate, volumetric_source_term, node_substance_label)

    if modes == 4 and space % 2 == 0 and space <= 2 * halo + 2:
        groups = space // 2
        fetched, swapped = [], []
        for step in range(groups):
            across = (2, 1, 3)[step] if step < 3 else 0
            moves = []
            for m in range(modes):
                for s in range(space):
                    source = (s - (m % 2) * groups - step) % space
                    moves.append(((m ^ across) * space + source, m * space + s))
            fetched.append(lax.ppermute(payload, ("modes", "space"), moves))
        for block in fetched:
            swapped.append(lax.ppermute(block, "modes", [(m, m ^ 1) for m in range(modes)]))
        blocks = [block for pair in zip(fetched, swapped) for block in pair]
        lookups = [payload] + fetched[:3]
        if groups < 3:
            lookups = [lax.psum(payload, "modes")]

        def places():
            m, s = lax.axis_index("modes"), lax.axis_index("space")
            core = lax.rem(m, 2)
            leads, swaps = [], []
            for step in range(groups):
                owner = lax.rem(s - core * groups - step + 2 * space, space)
                leads.append(lax.rem(owner, groups) * rows)
                swaps.append(owner >= groups)
            return leads, swaps, lax.rem(s, groups) * rows, s >= groups

    else:
        groups = halo + 1
        everything = lax.all_gather(payload, "space", axis=0, tiled=False)
        everything = jnp.pad(everything, ((halo, halo + 1), (0, 0), (0, 0), (0, 0)))
        first = lax.axis_index("space")
        near = lax.dynamic_slice_in_dim(everything, first, 2 * groups, 0)
        blocks = [near[at] for step in range(groups) for at in (step, step + groups)]
        lookups = [lax.psum(payload, "modes")]

        def places():
            return [step * rows for step in range(groups)], [False] * groups, halo * rows, False

    tables = pl.pallas_call(
        lambda *refs: table_kernel(modes, per_part, *refs),
        out_shape=jax.ShapeDtypeStruct((len(TABLES), 8, 128), jnp.float32),
        grid=(1,),
        in_specs=[pl.BlockSpec((1, 8, width), lambda i: (depth - 1, 0, 0)) for _ in lookups] + [vmem] * 5,
        out_specs=vmem,
        scratch_shapes=[
            pltpu.VMEM((8 * len(GROUPS), 128), jnp.float32),
            pltpu.VMEM((128 * COLUMN_TILES, 128), jnp.float32),
        ],
        name="tables",
    )(
        *lookups,
        propagation_velocity_table,
        specific_heat_table,
        collision_frequency_table.T,
        ordinate_inclination,
        ordinate_longitude,
    )
    length = groups * rows
    whole = length + 2 * REACH
    return pl.pallas_call(
        lambda *refs: main_kernel(groups, places, *refs),
        out_shape=(
            jax.ShapeDtypeStruct((planes, rows, tile), jnp.float32),
            jax.ShapeDtypeStruct((3, planes, rows, tile), jnp.float32),
        ),
        in_specs=[vmem] * (2 * groups + 1),
        out_specs=(vmem, vmem),
        scratch_shapes=[
            pltpu.VMEM((whole, 8, 128), jnp.float32),
            pltpu.VMEM((whole, 8, 128), jnp.float32),
            pltpu.VMEM((whole, 8, 128), jnp.int32),
            pltpu.VMEM((len(FAR), whole, 8, 128), jnp.float32),
            pltpu.VMEM((len(NEAR), whole, 8, 128), jnp.float32),
            pltpu.VMEM((len(NEAR), whole, 8, 128), jnp.int32),
            pltpu.VMEM((whole, 8, 128), jnp.float32),
            pltpu.VMEM((length, 8, 128), jnp.float32),
            pltpu.VMEM((rows, 8, 128), jnp.float32),
            pltpu.VMEM((7, length, 8, 128), jnp.float32),
            pltpu.VMEM((length, 8, 128), jnp.float32),
            pltpu.VMEM((2, length + 2, 8, 128), jnp.float32),
        ],
        compiler_params=pltpu.CompilerParams(vmem_limit_bytes=32 * 1024 * 1024),
        name="solve",
    )(*blocks, tables)


def solution(mesh):
    placed = (
        P(None, "space", None),
        P(None, "space", None),
        P(None, "space", None),
        P("modes"),
        P(),
        P(),
        P(),
        P(),
        P(),
    )
    return jax.shard_map(
        on_device,
        mesh=mesh,
        in_specs=placed,
        out_specs=(P(None, "space", "modes"), P(None, None, "space", "modes")),
        check_vma=False,
    )
```

```python
import itertools

import jax
import jax.numpy as jnp
from jax import lax
from jax.experimental import pallas as pl
from jax.experimental.pallas import tpu as pltpu
from jax.sharding import PartitionSpec as P


SWEEPS = 3
CHEB = 16
PART = 32
CODES = (0, 1, 3)
HIGHEST = lax.Precision.HIGHEST
APART = ((0, 1, 3, 6), (4, 2, 5, 7))


def monomials(degree):
    found = []
    for axes in itertools.combinations_with_replacement(range(3), degree):
        distinct = sorted(set(axes))
        for rest in itertools.product((-1, 1), repeat=max(len(distinct) - 1, 0)):
            found.append((axes, tuple(zip(distinct, (-1,) + rest)) if distinct else ()))
    return found


MONO = {degree: monomials(degree) for degree in range(4)}


def canonical(steps):
    axes = tuple(sorted(axis for axis, _ in steps))
    signs = dict(steps)
    first = signs[axes[0]]
    pattern = tuple((axis, signs[axis] * -first) for axis in sorted(signs))
    return (axes, pattern), -first


PAIRS = {CODES[a] + CODES[b]: [(1, (a, b))] for a, b in itertools.combinations_with_replacement(range(3), 2)}
TRIPLES = {
    CODES[a] + CODES[b] + CODES[c]: [(1, (a, b, c))]
    for a, b, c in itertools.combinations_with_replacement(range(3), 3)
    if (a, b, c) not in ((1, 1, 1), (2, 2, 2))
}
SINGLES = {CODES[a]: [(1, (a,))] for a in range(3)}
ALIKE = {1: 5, 2: 7}
PAIRS_ALIKE = dict(PAIRS)
EXTRA = {}
for label, place in ALIKE.items():
    PAIRS_ALIKE[place] = [(1, (label, label))]
    EXTRA[place] = [(-1, (label,) * 3)] + TRIPLES[(3 * CODES[label]) & 7]
GROUPS = {
    "u3": (3, False, PAIRS_ALIKE),
    "u2": (2, False, PAIRS_ALIKE),
    "u1d": (2, False, SINGLES),
    "u1": (1, False, SINGLES),
    "u0d": (1, True, SINGLES),
    "u0": (0, True, SINGLES),
    "a3": (4, False, TRIPLES),
    "x3": (4, False, EXTRA),
    "a2": (3, False, TRIPLES),
    "x2": (3, False, EXTRA),
    "v1d": (3, False, PAIRS),
    "v1": (2, False, PAIRS),
    "f0d": (2, False, SINGLES),
}
GROUP_AT = {name: at for at, name in enumerate(GROUPS)}
COLUMNS = (
    [("u", degree, mono) for degree in (3, 2, 1, 0) for mono in MONO[degree]]
    + [("v", degree, mono) for degree in (3, 2, 1) for mono in MONO[degree]]
    + [(axis, degree, mono) for axis in range(3) for degree in (3, 2, 1) for mono in MONO[degree]]
)
COLUMN_AT = {column: at for at, column in enumerate(COLUMNS)}
COLUMN_TILES = -(-len(COLUMNS) // 128)


def table_list():
    found = [("inverse_rate",), ("conduct",), ("inverse_theta",)]
    found += [("keep", step) for step in range(CHEB - 1)] + [("gain", step) for step in range(CHEB - 1)]
    for group, degree in (("u3", 3), ("u2", 2), ("u1d", 2), ("u1", 1), ("u0d", 1), ("u0", 0)):
        found += [(group, "u", degree, mono) for mono in MONO[degree]]
    for kind in ("v", 0, 1, 2):
        for group, degree in (("a3", 3), ("x3", 3), ("a2", 2), ("x2", 2), ("v1d", 2), ("v1", 1)):
            if kind == "v" and group[0] == "x":
                continue
            found += [(group, kind, degree, mono) for mono in MONO[degree]]
    for kind in (0, 1, 2):
        found += [("f0d", kind, 1, mono) for mono in MONO[1]]
    return found


TABLES = table_list()
TABLE_AT = {key: at for at, key in enumerate(TABLES)}


def lanes(shape):
    return lax.broadcasted_iota(jnp.int32, shape, len(shape) - 1)


def sublanes(shape):
    return lax.broadcasted_iota(jnp.int32, shape, len(shape) - 2)


def pack_kernel(*refs):
    inputs, (out_ref, small_ref), held, sems = refs[:9], refs[9:11], refs[11:20], refs[20]
    copies = [pltpu.make_async_copy(source, to, sems.at[at]) for at, (source, to) in enumerate(zip(inputs, held))]
    for copy in copies:
        copy.start()
    values_ref, source_ref, label_ref, lookup_ref, velocity_ref, heat_ref, rate_ref, polar_ref, azimuth_ref = held
    planes, rows, _ = values_ref.shape
    part = rows * planes // 8
    lane = lanes(out_ref.shape[1:])
    copies[3].wait()
    found = jnp.zeros(out_ref.shape[1:], jnp.int32)
    for at in range(lookup_ref.shape[0]):
        found = jnp.where(lane == at, lookup_ref[at] + 1, found)
    out_ref[3 * part] = found.astype(jnp.float32)
    for which, ref in enumerate((values_ref, source_ref, label_ref)):
        copies[which].wait()
        for plane in range(planes):
            for row in range(rows):
                at, sub = divmod(row * planes + plane, 8)
                value = ref[plane, row : row + 1, :]
                if which == 2:
                    value = (value + 1).astype(jnp.float32)
                out_ref[which * part + at, sub : sub + 1, :] = value
    small_ref[...] = jnp.zeros(small_ref.shape, jnp.float32)
    for copy in copies[4:]:
        copy.wait()
    size, half_dir = velocity_ref.shape[0], polar_ref.shape[0]
    small_ref[0, 0:size] = velocity_ref[...]
    small_ref[1, 0:size] = heat_ref[...]
    small_ref[2:5, 0:size] = rate_ref[...]
    for start in range(0, 128, PART):
        small_ref[8, start : start + half_dir] = polar_ref[...]
        small_ref[9, start : start + half_dir] = azimuth_ref[...]


def table_kernel(parts, per_part, half_dir, *refs):
    lookups = refs[:-4]
    small_ref, out_ref, work_ref, axes_ref = refs[-4:]
    padded = -(-per_part // 8) * 8
    lane = lanes((1, 128))

    last = lookups[0].shape[0] - 1
    modes = lax.axis_index("modes")
    found = jnp.zeros((1, 128), jnp.float32)
    owner = jnp.zeros((1, 128), jnp.int32)
    for part, ref in enumerate(lookups):
        row = ref[last, 0:1, 0:128]
        found = found + (pltpu.roll(row, part * PART, axis=1) if part else row)
        owner = jnp.where(lane // PART == part, modes ^ part, owner)
    index = found.astype(jnp.int32) - 1
    valid = index >= 0
    index = jnp.broadcast_to(jnp.where(valid, index, 0), (8, 128))
    picked = jnp.take_along_axis(small_ref[0:8, :], index, axis=1, mode="promise_in_bounds")
    frequency = owner * per_part + lane % PART
    spectral = (frequency.astype(jnp.float32) + 1.0) / (parts * per_part)
    velocity = jnp.where(valid, picked[0:1], 1.0)
    capacity = jnp.where(valid, picked[1:2] * spectral, 0.0)
    rates = [jnp.where(valid, picked[2 + k : 3 + k], 1.0) for k in range(3)]

    conducts, inverses = [], []
    for k in range(3):
        rate_total = jnp.sum(capacity * rates[k], axis=1, keepdims=True)
        cond_total = jnp.sum(capacity * velocity * velocity / (3.0 * rates[k]), axis=1, keepdims=True)
        conducts.append(cond_total / rate_total)
        inverses.append(1.0 / (2 * half_dir * rate_total))
    sub = sublanes((8, 128))

    def by_label(values):
        found = jnp.zeros((8, 128), jnp.float32)
        for code, value in zip(CODES, values):
            found = jnp.where(sub == code, value, found)
        return found

    out_ref[TABLE_AT["inverse_rate",]] = by_label(inverses)
    out_ref[TABLE_AT["conduct",]] = by_label(conducts)
    top = 1.0 + 12.0 * jnp.maximum(jnp.maximum(conducts[0], conducts[1]), conducts[2])
    top = jnp.broadcast_to(top, (8, 128))
    theta = (top + 1.0) / 2.0
    delta = (top - 1.0) / 2.0
    sigma = theta / delta
    rho = 1.0 / sigma
    out_ref[TABLE_AT["inverse_theta",]] = 1.0 / theta
    for step in range(CHEB - 1):
        rho_new = 1.0 / (2.0 * sigma - rho)
        out_ref[TABLE_AT["keep", step]] = rho_new * rho
        out_ref[TABLE_AT["gain", step]] = 2.0 * rho_new / delta
        rho = rho_new

    angles = small_ref[8:16, :]
    cosines, sines = jnp.cos(angles), jnp.sin(angles)
    real = (lane % PART) < half_dir
    u = [cosines[0:1], sines[0:1] * cosines[1:2], sines[0:1] * sines[1:2]]
    u = [jnp.where(real, part, 0.0) for part in u]
    a = [jnp.abs(part) for part in u]
    total = a[0] + a[1] + a[2]
    sides = [jnp.where(part >= 0.0, 1.0, -1.0) for part in u]

    products = {(): jnp.where(real, 1.0, 0.0)}
    for degree in (1, 2, 3):
        for axes in itertools.combinations_with_replacement(range(3), degree):
            products[axes] = products[axes[:-1]] * a[axes[-1]]
    masks = {}
    for degree in range(4):
        for _, pattern in MONO[degree]:
            if pattern not in masks:
                same = flipped = jnp.ones((1, 128), jnp.float32)
                for axis, sign in pattern:
                    if axis == 0:
                        flipped = jnp.zeros((1, 128), jnp.float32)
                    else:
                        same = same * jnp.where(sides[axis] == -sign, 1.0, 0.0)
                        flipped = flipped * jnp.where(sides[axis] == sign, 1.0, 0.0)
                masks[pattern] = (same + flipped, same - flipped)
    axes_ref[...] = jnp.zeros(axes_ref.shape, jnp.float32)
    weights = {"u": None, "v": total}
    weights.update({axis: u[axis] * (1.0 / (2 * half_dir)) for axis in range(3)})
    for at, (kind, degree, (axes, pattern)) in enumerate(COLUMNS):
        even, odd = masks[pattern]
        row = products[axes] * (even if kind in ("u", "v") else odd)
        if weights[kind] is not None:
            row = row * weights[kind]
        axes_ref[at : at + 1, :] = row

    columns = jnp.concatenate([velocity, capacity] + rates + [jnp.zeros((3, 128), jnp.float32)], axis=0).T

    def spread(at):
        found = jnp.zeros((padded, 128), jnp.float32)
        where = lanes((padded, 128)) // PART
        for part in range(parts):
            column = columns[part * PART : part * PART + padded, at : at + 1]
            found = jnp.where(where == part, column, found)
        return found

    speed, stored = spread(0), spread(1)
    loss = [spread(2 + k) for k in range(3)]
    inverse = [1.0 / (speed * total + loss[k]) for k in range(3)]
    weight = [stored]
    for _ in range(4):
        weight.append(weight[-1] * speed)
    chains = {}
    for length in (1, 2, 3):
        for labels in itertools.combinations_with_replacement(range(3), length):
            chains[labels] = inverse[labels[0]] if length == 1 else chains[labels[:-1]] * inverse[labels[-1]]
    work_ref[...] = jnp.zeros(work_ref.shape, jnp.float32)
    for name, (power, rated, index) in GROUPS.items():
        for code, terms in index.items():
            field = sum(sign * chains[tuple(sorted(labels))] for sign, labels in terms) * weight[power]
            if rated:
                field = field * loss[terms[0][1][0]]
            at = GROUP_AT[name] * 8 + code
            work_ref[at : at + 1, :] = jnp.sum(field, axis=0, keepdims=True)
    sums = lax.dot_general(
        work_ref[...],
        axes_ref[...],
        (((1,), (1,)), ((), ())),
        precision=HIGHEST,
        preferred_element_type=jnp.float32,
    )
    for at, key in enumerate(TABLES):
        if len(key) == 4:
            row, column = GROUP_AT[key[0]] * 8, COLUMN_AT[key[1:]]
            values = sums[row : row + 8, column : column + 1]
            if key[0] in ("u3", "u2"):
                row, column = GROUP_AT["x" + key[0][1]] * 8, COLUMN_AT[("v",) + key[2:]]
                values = values + sums[row : row + 8, column : column + 1]
            out_ref[at] = jnp.broadcast_to(values, (8, 128))


SIGNED = [(axis, sign) for axis in range(3) for sign in (-1, 1)]


def follows(earlier, step):
    return all((step[0], -step[1]) != before for before in earlier)


def displacement(steps):
    found = [0, 0, 0]
    for axis, sign in steps:
        found[axis] += sign
    return tuple(found)


def ends_of_two():
    found = {}
    for first in SIGNED:
        for second in SIGNED:
            if follows((first,), second):
                found.setdefault(tuple(sorted((first, second))), []).append(first)
    return found


ENDS = ends_of_two()
REACH = SWEEPS
FAR = [(z, y) for z in range(-3, 4) for y in range(-3, 4) if abs(z) + abs(y) <= 3]
NEAR = [(z, y) for z in range(-2, 3) for y in range(-2, 3) if abs(z) + abs(y) <= 2]
FAR_AT = {key: at for at, key in enumerate(FAR)}
NEAR_AT = {key: at for at, key in enumerate(NEAR)}


def pick(table, index):
    return jnp.take_along_axis(table, index, axis=0, mode="promise_in_bounds")


class Cells:
    def __init__(self, entry, far_ref, source_ref, code_ref):
        self.entry = entry
        self.refs = (far_ref, source_ref, code_ref)
        self.known = {}

    def get(self, which, place):
        key = (which, place)
        if key not in self.known:
            x, y, z = place
            at = FAR_AT[z, y] if which == 0 else NEAR_AT[z, y]
            self.known[key] = self.refs[which][at, self.entry + REACH + x]
        return self.known[key]

    def code(self):
        if "alike" not in self.known:
            code = self.get(2, (0, 0, 0))
            expected = jnp.where(code == CODES[0], -1, 2 * code)
            self.known["alike"] = (expected, jnp.where(code == CODES[1], ALIKE[1], ALIKE[2]))
        return self.known["alike"]

    def rise(self, place, step):
        further = list(place)
        further[step[0]] += step[1]
        return self.get(0, tuple(further)) - self.get(0, place)


class Pairs(Cells):
    def __init__(self, entry, shift, raw, far_ref, source_ref, code_ref):
        super().__init__(entry, far_ref, source_ref, code_ref)
        self.shift, self.raw = shift, raw

    def get(self, which, place):
        key = (which, place)
        if key not in self.known:
            x, y, z = place
            at = FAR_AT[z, y] if which == 0 else NEAR_AT[z, y]
            ref = self.refs[which]
            straight = ref[at, self.entry + (REACH + x) + self.shift]
            turned = ref[at, self.entry + (REACH + x + self.apart) - self.shift]
            self.known[key] = jnp.where(self.raw, straight, pltpu.roll(turned, self.planes, axis=0))
        return self.known[key]


def alike(pair, code):
    expected, place = code
    return jnp.where(pair == expected, place, pair)


class Sums:
    def __init__(self, count=4):
        self.parts = [None] * count
        self.at = 0

    def add(self, value):
        held = self.parts[self.at]
        self.parts[self.at] = value if held is None else held + value
        self.at = (self.at + 1) % len(self.parts)

    def total(self):
        held = [part for part in self.parts if part is not None]
        while len(held) > 1:
            held = [sum(held[at + 1 : at + 2], held[at]) for at in range(0, len(held), 2)]
        return held[0]


def energy_of(cells_list, table):
    sums = [Sums() for _ in cells_list]
    here = (0, 0, 0)
    codes = [cells.get(2, here) for cells in cells_list]
    rest = table(("u0", "u", 0, MONO[0][0]))
    for cells, code, held in zip(cells_list, codes, sums):
        held.add(pick(rest, code) * cells.get(1, here))
    for step in SIGNED:
        mono, _ = canonical((step,))
        rest = table(("u0d", "u", 1, mono))
        for cells, code, held in zip(cells_list, codes, sums):
            held.add(pick(rest, code) * cells.rise(here, step))
    two = {}
    for first in SIGNED:
        place = displacement((first,))
        mono, _ = canonical((first,))
        nears = [cells.get(2, place) for cells in cells_list]
        two[first] = pairs = [near + code for near, code in zip(nears, codes)]
        one, other = table(("u1", "u", 1, mono)), table(("v1", "v", 1, mono))
        for cells, near, pair, held in zip(cells_list, nears, pairs, sums):
            held.add((pick(one, near) - pick(other, pair)) * cells.get(1, place))
        for step in SIGNED:
            if follows((first,), step):
                mono, _ = canonical((first, step))
                one, other = table(("u1d", "u", 2, mono)), table(("v1d", "v", 2, mono))
                for cells, near, pair, held in zip(cells_list, nears, pairs, sums):
                    held.add((pick(one, near) - pick(other, pair)) * cells.rise(place, step))
    for steps, firsts in ENDS.items():
        place = displacement(steps)
        index = []
        for at, cells in enumerate(cells_list):
            end = cells.get(2, place)
            mine = []
            for first in firsts:
                pair = cells.get(2, displacement((first,))) + end
                mine.append((alike(pair, cells.code()), (pair + codes[at]) & 7))
            index.append(mine)
        cases = [(None, "2", canonical(steps)[0], 2)]
        cases += [(step, "3", canonical(steps + (step,))[0], 3) for step in SIGNED if follows(steps, step)]
        for step, which, mono, degree in cases:
            one, other = table(("u" + which, "u", degree, mono)), table(("a" + which, "v", degree, mono))
            for cells, mine, held in zip(cells_list, index, sums):
                factor = None
                for pair, triple in mine:
                    term = pick(one, pair) - pick(other, triple)
                    factor = term if factor is None else factor + term
                held.add(factor * (cells.get(1, place) if step is None else cells.rise(place, step)))
    return [held.total() for held in sums]


def flux_of(cells, table):
    sums = [Sums(2) for _ in range(3)]
    here = (0, 0, 0)
    code = cells.get(2, here)

    def signed(value, side):
        return value if side > 0 else -value

    for step in SIGNED:
        mono, side = canonical((step,))
        rise = signed(cells.rise(here, step), side)
        for axis in range(3):
            sums[axis].add(pick(table(("f0d", axis, 1, mono)), code) * rise)
    for first in SIGNED:
        place = displacement((first,))
        pair = cells.get(2, place) + code
        mono, side = canonical((first,))
        value = signed(cells.get(1, place), side)
        for axis in range(3):
            sums[axis].add(pick(table(("v1", axis, 1, mono)), pair) * value)
        for step in SIGNED:
            if follows((first,), step):
                mono, side = canonical((first, step))
                value = signed(cells.rise(place, step), side)
                for axis in range(3):
                    sums[axis].add(pick(table(("v1d", axis, 2, mono)), pair) * value)
    for steps, firsts in ENDS.items():
        place = displacement(steps)
        end = cells.get(2, place)
        index = []
        for first in firsts:
            pair = cells.get(2, displacement((first,))) + end
            index.append((alike(pair, cells.code()), (pair + code) & 7))
        cases = [(None, "2", canonical(steps), 2)]
        cases += [(step, "3", canonical(steps + (step,)), 3) for step in SIGNED if follows(steps, step)]
        for step, which, (mono, side), degree in cases:
            value = signed(cells.get(1, place) if step is None else cells.rise(place, step), side)
            for axis in range(3):
                one, other = table(("a" + which, axis, degree, mono)), table(("x" + which, axis, degree, mono))
                factor = None
                for pair, triple in index:
                    term = pick(one, triple) - pick(other, pair)
                    factor = term if factor is None else factor + term
                sums[axis].add(factor * value)
    return [held.total() for held in sums]


def main_kernel(groups, places, *refs):
    blocks = refs[: 2 * groups]
    table_ref, temperature_ref, flux_ref, base_ref, source_base_ref, code_base_ref = refs[2 * groups : 2 * groups + 6]
    far_ref, near_ref, code_ref, kappa_ref, force_ref, coef_ref, mismatch_ref, first_ref, second_ref = refs[
        2 * groups + 6 :
    ]
    planes, rows, tile = temperature_ref.shape
    width = blocks[0].shape[2]
    parts = rows * planes // 8
    length = groups * rows
    lane, sub = lanes((8, 128)), sublanes((8, 128))
    lower = sub < planes
    wide_lower = sublanes((8, width)) < planes
    plane = sub % planes
    modes = lax.axis_index("modes")
    leads, swaps, others, core_first, own_lead, own_upper = places()

    margin = (128 - tile) // 2
    start = modes * tile - margin
    column = start + lane
    inside = (column >= 0) & (column < width)
    left = (start + 128) // 128 - 1
    turn = 128 - (start - left * 128)
    from_first = (lane >= 128 - turn) == (lax.rem(left + 2, 2) == 0)

    def window(wide):
        return pltpu.roll(jnp.where(from_first, wide[:, 0:128], wide[:, 128:256]), turn, axis=1)

    for group in range(groups):
        one, (two, other) = blocks[group], [blocks[groups + at] for at in others[group]]
        swap = swaps[group]
        for which, ref in enumerate((base_ref, source_base_ref, code_base_ref)):
            for part in range(parts):
                first, second = one[which * parts + part], two[which * parts + part]
                if other is not two:
                    second = jnp.where(core_first, second, other[which * parts + part])
                low, high = jnp.where(swap, second, first), jnp.where(swap, first, second)
                pair = (
                    window(jnp.where(wide_lower, low, pltpu.roll(high, planes, axis=0))),
                    window(jnp.where(wide_lower, pltpu.roll(low, planes, axis=0), high)),
                )
                for row in range(2):
                    at = REACH + leads[group] + 2 * part + row
                    if which < 2:
                        ref[at] = jnp.where(inside, pair[row], 0.0)
                    else:
                        ref[at] = jnp.where(inside, pair[row], 0.0).astype(jnp.int32)

    for ref in (base_ref, source_base_ref, code_base_ref):
        none = jnp.zeros((8, 128), ref.dtype)
        for at in range(REACH):
            ref[at] = jnp.where(lower, none, pltpu.roll(ref[at + length], planes, axis=0))
            ref[length + REACH + at] = jnp.where(lower, pltpu.roll(ref[REACH + at], planes, axis=0), none)

    conduct = table_ref[TABLE_AT["conduct",]]

    def shift_plane(value, z, none):
        if z == 0:
            return value
        return jnp.where((plane + z >= 0) & (plane + z < planes), pltpu.roll(value, (-z) % 8, axis=0), none)

    def spread(reach, value, out, keys, at, masked):
        beyond = max(REACH - at, at - (REACH + length - 1), 0)
        for y in sorted({y for _, y in keys}):
            if abs(y) + beyond > reach:
                continue
            moved = pltpu.roll(value, (-y) % 128, axis=1) if y else value
            for z in sorted({z for z, other in keys if other == y}):
                if abs(y) + abs(z) + beyond > reach:
                    continue
                if masked:
                    out[keys[z, y], at] = shift_plane(moved, z, 0.0)
                else:
                    out[keys[z, y], at] = pltpu.roll(moved, (-z) % 8, axis=0) if z else moved

    for at in range(length + 2 * REACH):
        spread(3, base_ref[at], far_ref, FAR_AT, at, True)
        spread(2, source_base_ref[at], near_ref, NEAR_AT, at, True)
        label = code_base_ref[at]
        kind = jnp.maximum(label - 1, 0)
        code = jnp.where(kind == 2, CODES[2], kind)
        kappa_ref[at] = jnp.where(label > 0, pick(conduct, code), 0.0)
        spread(2, code, code_ref, NEAR_AT, at, False)

    def table(key):
        return table_ref[TABLE_AT[key]]

    def forcing(step, _):
        entries = (2 * step, 2 * step + 1)
        cells_list = [Cells(entry, far_ref, near_ref, code_ref) for entry in entries]
        energies = energy_of(cells_list, table)
        scale = table_ref[TABLE_AT["inverse_rate",]]
        for entry, cells, energy in zip(entries, cells_list, energies):
            force = energy * pick(scale, cells.get(2, (0, 0, 0)))
            force_ref[entry] = jnp.where(code_base_ref[entry + REACH] > 0, force, 0.0)
        return 0

    lax.fori_loop(0, length // 2, forcing, 0)

    none = jnp.zeros((8, 128), jnp.float32)
    inverse_theta = table_ref[TABLE_AT["inverse_theta",]]
    for entry in range(length):
        kappa = kappa_ref[entry + REACH]
        real = code_base_ref[entry + REACH] > 0
        others = [
            kappa_ref[entry + REACH - 1],
            kappa_ref[entry + REACH + 1],
            pltpu.roll(kappa, 1, axis=1),
            pltpu.roll(kappa, 127, axis=1),
            shift_plane(kappa, -1, 0.0),
            shift_plane(kappa, 1, 0.0),
        ]
        faces = [jnp.where(real, 0.5 * (kappa + other), 0.0) for other in others]
        coef_ref[6, entry] = 1.0 + ((faces[0] + faces[1]) + (faces[2] + faces[3]) + (faces[4] + faces[5]))
        faces[4] = jnp.where(plane >= 1, faces[4], 0.0)
        faces[5] = jnp.where(plane < planes - 1, faces[5], 0.0)
        for at in range(6):
            coef_ref[at, entry] = faces[at]
        mismatch_ref[entry] = force_ref[entry]
        first_ref[entry + 1] = force_ref[entry] * inverse_theta

    def edges(ref):
        ref[0] = jnp.where(lower, none, pltpu.roll(ref[length], planes, axis=0))
        ref[length + 1] = jnp.where(lower, pltpu.roll(ref[1], planes, axis=0), none)

    edges(first_ref)
    correction = [first_ref[own_lead + row + 1] for row in range(rows)]
    for step in range(CHEB - 1):
        old_ref, new_ref = (first_ref, second_ref) if step % 2 == 0 else (second_ref, first_ref)
        keep = table_ref[TABLE_AT["keep", step]]
        gain = table_ref[TABLE_AT["gain", step]]
        for entry in range(length):
            value = old_ref[entry + 1]
            flow = coef_ref[6, entry] * value - coef_ref[0, entry] * old_ref[entry]
            flow = flow - coef_ref[1, entry] * old_ref[entry + 2]
            side = coef_ref[2, entry] * pltpu.roll(value, 1, axis=1)
            side = side + coef_ref[3, entry] * pltpu.roll(value, 127, axis=1)
            deep = coef_ref[4, entry] * pltpu.roll(value, 1, axis=0)
            deep = deep + coef_ref[5, entry] * pltpu.roll(value, 7, axis=0)
            mismatch = mismatch_ref[entry] - (flow - (side + deep))
            if step < CHEB - 2:
                mismatch_ref[entry] = mismatch
            new_ref[entry + 1] = keep * value + gain * mismatch
        if step < CHEB - 2:
            edges(new_ref)
        correction = [held + new_ref[own_lead + row + 1] for row, held in enumerate(correction)]

    def cut(value):
        value = jnp.where(own_upper, pltpu.roll(value, planes, axis=0), value)
        return pltpu.roll(value, 128 - margin, axis=1)[0:planes, 0:tile]

    for row in range(rows):
        entry = own_lead + row
        found = cut(base_ref[entry + REACH] + force_ref[entry] + correction[row])
        for at in range(planes):
            temperature_ref[at, row : row + 1, :] = found[at : at + 1]

    paired = rows // 2
    upper = jnp.where(own_upper, 1, 0)
    raw = jnp.where(lower, 0, 1) == upper

    def fluxes(row, _):
        cells = Pairs(own_lead + row, upper * paired, raw, far_ref, near_ref, code_ref)
        cells.planes, cells.apart = planes, paired
        for axis, found in enumerate(flux_of(cells, table)):
            coef_ref[axis, row] = found
        return 0

    lax.fori_loop(0, paired, fluxes, 0)
    for axis in range(3):
        for row in range(paired):
            found = pltpu.roll(coef_ref[axis, row], 128 - margin, axis=1)[:, 0:tile]
            for half in range(2):
                for at in range(planes):
                    line = half * planes + at
                    place = row + half * paired
                    flux_ref[axis, at, place : place + 1, :] = found[line : line + 1]


def on_device(
    thermal_deviation_iterate,
    volumetric_source_term,
    node_substance_label,
    spectral_table_lookup,
    propagation_velocity_table,
    specific_heat_table,
    collision_frequency_table,
    ordinate_inclination,
    ordinate_longitude,
):
    planes, rows, width = thermal_deviation_iterate.shape
    modes, space = lax.axis_size("modes"), lax.axis_size("space")
    tile = width // modes
    per_part = spectral_table_lookup.shape[0]
    half_dir = ordinate_inclination.shape[0]
    assert planes * 2 == 8 and rows % 2 == 0 and width == 256
    assert modes in (1, 2, 4) and per_part <= PART and half_dir <= PART
    halo = -(-(CHEB - 1 + SWEEPS) // rows)
    reach = CHEB - 1 + SWEEPS
    assert tile + 2 * reach <= 128
    vmem = pl.BlockSpec(memory_space=pltpu.VMEM)
    parts = rows * planes // 8
    depth = 3 * parts + 1
    arguments = (
        thermal_deviation_iterate,
        volumetric_source_term,
        node_substance_label,
        spectral_table_lookup,
        propagation_velocity_table,
        specific_heat_table,
        collision_frequency_table.T,
        ordinate_inclination,
        ordinate_longitude,
    )
    held = [(pltpu.SMEM if at == 3 else pltpu.VMEM)(x.shape, x.dtype) for at, x in enumerate(arguments)]
    payload, small = pl.pallas_call(
        pack_kernel,
        out_shape=(pltpu.VMEM((depth, 8, width), jnp.float32), pltpu.VMEM((16, 128), jnp.float32)),
        in_specs=[pl.BlockSpec(memory_space=pltpu.HBM)] * len(arguments),
        out_specs=(vmem, vmem),
        scratch_shapes=held + [pltpu.SemaphoreType.DMA((len(arguments),))],
        name="pack",
    )(*arguments)

    if modes == 4 and space == 8:
        groups = 4
        fetched, swapped = [], []
        for apart, across in zip(zip(*APART), (2, 0, 0, 0)):
            moves = []
            for m in range(modes):
                for s in range(space):
                    moves.append(((m ^ across) * space + (s ^ apart[m % 2]), m * space + s))
            fetched.append(lax.ppermute(payload, ("modes", "space"), moves))
        for block in fetched:
            swapped.append(lax.ppermute(block, "modes", [(m, m ^ 1) for m in range(modes)]))
        blocks = fetched + swapped
        lookups = [payload, swapped[1], fetched[0], swapped[0]]

        def places():
            m, s = lax.axis_index("modes"), lax.axis_index("space")
            core = lax.rem(m, 2)
            leads, swaps, others = [], [], []
            for step in range(groups):
                owner = s ^ jnp.where(core == 0, APART[0][step], APART[1][step])
                leads.append(lax.rem(owner, groups) * rows)
                swaps.append(owner >= groups)
                others.append([APART[1 - c].index(APART[c][step] ^ groups) for c in range(2)])
            return leads, swaps, others, core == 0, lax.rem(s, groups) * rows, s >= groups

    else:
        groups = halo + 1
        everything = lax.all_gather(payload, "space", axis=0, tiled=False)
        everything = jnp.pad(everything, ((halo, halo + 1), (0, 0), (0, 0), (0, 0)))
        first = lax.axis_index("space")
        near = lax.dynamic_slice_in_dim(everything, first, 2 * groups, 0)
        blocks = [near[at] for at in range(2 * groups)]
        lookups = [payload]
        for apart in range(1, modes):
            lookups.append(lax.ppermute(payload, "modes", [(m, m ^ apart) for m in range(modes)]))

        def places():
            same = [[step, step] for step in range(groups)]
            return [step * rows for step in range(groups)], [False] * groups, same, True, halo * rows, False

    tables = pl.pallas_call(
        lambda *refs: table_kernel(modes, per_part, half_dir, *refs),
        out_shape=pltpu.VMEM((len(TABLES), 8, 128), jnp.float32),
        in_specs=[vmem] * (len(lookups) + 1),
        out_specs=vmem,
        compiler_params=pltpu.CompilerParams(vmem_limit_bytes=8 * 1024 * 1024),
        scratch_shapes=[
            pltpu.VMEM((8 * len(GROUPS), 128), jnp.float32),
            pltpu.VMEM((128 * COLUMN_TILES, 128), jnp.float32),
        ],
        name="tables",
    )(
        *lookups,
        small,
    )
    length = groups * rows
    whole = length + 2 * REACH
    return pl.pallas_call(
        lambda *refs: main_kernel(groups, places, *refs),
        out_shape=(
            jax.ShapeDtypeStruct((planes, rows, tile), jnp.float32),
            jax.ShapeDtypeStruct((3, planes, rows, tile), jnp.float32),
        ),
        in_specs=[vmem] * (2 * groups + 1),
        out_specs=(vmem, vmem),
        scratch_shapes=[
            pltpu.VMEM((whole, 8, 128), jnp.float32),
            pltpu.VMEM((whole, 8, 128), jnp.float32),
            pltpu.VMEM((whole, 8, 128), jnp.int32),
            pltpu.VMEM((len(FAR), whole, 8, 128), jnp.float32),
            pltpu.VMEM((len(NEAR), whole, 8, 128), jnp.float32),
            pltpu.VMEM((len(NEAR), whole, 8, 128), jnp.int32),
            pltpu.VMEM((whole, 8, 128), jnp.float32),
            pltpu.VMEM((length, 8, 128), jnp.float32),
            pltpu.VMEM((7, length, 8, 128), jnp.float32),
            pltpu.VMEM((length, 8, 128), jnp.float32),
            pltpu.VMEM((length + 2, 8, 128), jnp.float32),
            pltpu.VMEM((length + 2, 8, 128), jnp.float32),
        ],
        compiler_params=pltpu.CompilerParams(vmem_limit_bytes=32 * 1024 * 1024),
        name="solve",
    )(*blocks, tables)


def solution(mesh):
    placed = (
        P(None, "space", None),
        P(None, "space", None),
        P(None, "space", None),
        P("modes"),
        P(),
        P(),
        P(),
        P(),
        P(),
    )
    return jax.shard_map(
        on_device,
        mesh=mesh,
        in_specs=placed,
        out_specs=(P(None, "space", "modes"), P(None, None, "space", "modes")),
        check_vma=False,
    )
```

```python
import itertools

import jax
import jax.numpy as jnp
from jax import lax
from jax.experimental import pallas as pl
from jax.experimental.pallas import tpu as pltpu
from jax.sharding import PartitionSpec as P


SWEEPS = 3
CHEB = 16
REACH_COLUMNS = SWEEPS + CHEB - 1
PART = 32
CODES = (0, 1, 3)
HIGHEST = lax.Precision.HIGHEST
APART = ((1, 3, 6), (2, 5, 7))
APART_BOTH = 4


def monomials(degree):
    found = []
    for axes in itertools.combinations_with_replacement(range(3), degree):
        distinct = sorted(set(axes))
        for rest in itertools.product((-1, 1), repeat=max(len(distinct) - 1, 0)):
            found.append((axes, tuple(zip(distinct, (-1,) + rest)) if distinct else ()))
    return found


MONO = {degree: monomials(degree) for degree in range(4)}


def canonical(steps):
    axes = tuple(sorted(axis for axis, _ in steps))
    signs = dict(steps)
    first = signs[axes[0]]
    pattern = tuple((axis, signs[axis] * -first) for axis in sorted(signs))
    return (axes, pattern), -first


PAIRS = {CODES[a] + CODES[b]: [(1, (a, b))] for a, b in itertools.combinations_with_replacement(range(3), 2)}
TRIPLES = {
    CODES[a] + CODES[b] + CODES[c]: [(1, (a, b, c))]
    for a, b, c in itertools.combinations_with_replacement(range(3), 3)
    if (a, b, c) not in ((1, 1, 1), (2, 2, 2))
}
SINGLES = {CODES[a]: [(1, (a,))] for a in range(3)}
ALIKE = {1: 5, 2: 7}
PAIRS_ALIKE = dict(PAIRS)
EXTRA = {}
for label, place in ALIKE.items():
    PAIRS_ALIKE[place] = [(1, (label, label))]
    EXTRA[place] = [(-1, (label,) * 3)] + TRIPLES[(3 * CODES[label]) & 7]
GROUPS = {
    "u3": (3, False, PAIRS_ALIKE),
    "u2": (2, False, PAIRS_ALIKE),
    "u1d": (2, False, SINGLES),
    "u1": (1, False, SINGLES),
    "u0d": (1, True, SINGLES),
    "u0": (0, True, SINGLES),
    "a3": (4, False, TRIPLES),
    "x3": (4, False, EXTRA),
    "a2": (3, False, TRIPLES),
    "x2": (3, False, EXTRA),
    "v1d": (3, False, PAIRS),
    "v1": (2, False, PAIRS),
    "f0d": (2, False, SINGLES),
}
GROUP_AT = {name: at for at, name in enumerate(GROUPS)}
COLUMNS = (
    [("u", degree, mono) for degree in (3, 2, 1, 0) for mono in MONO[degree]]
    + [("v", degree, mono) for degree in (3, 2, 1) for mono in MONO[degree]]
    + [(axis, degree, mono) for axis in range(3) for degree in (3, 2, 1) for mono in MONO[degree]]
)
COLUMN_AT = {column: at for at, column in enumerate(COLUMNS)}
COLUMN_TILES = -(-len(COLUMNS) // 128)


def table_list():
    found = [("inverse_rate",), ("conduct",), ("inverse_theta",)]
    found += [("keep", step) for step in range(CHEB - 1)] + [("gain", step) for step in range(CHEB - 1)]
    for group, degree in (("u3", 3), ("u2", 2), ("u1d", 2), ("u1", 1), ("u0d", 1), ("u0", 0)):
        found += [(group, "u", degree, mono) for mono in MONO[degree]]
    for kind in ("v", 0, 1, 2):
        for group, degree in (("a3", 3), ("x3", 3), ("a2", 2), ("x2", 2), ("v1d", 2), ("v1", 1)):
            if kind == "v" and group[0] == "x":
                continue
            found += [(group, kind, degree, mono) for mono in MONO[degree]]
    for kind in (0, 1, 2):
        found += [("f0d", kind, 1, mono) for mono in MONO[1]]
    return found


TABLES = table_list()
TABLE_AT = {key: at for at, key in enumerate(TABLES)}


def lanes(shape):
    return lax.broadcasted_iota(jnp.int32, shape, len(shape) - 1)


def sublanes(shape):
    return lax.broadcasted_iota(jnp.int32, shape, len(shape) - 2)


def pack_kernel(*refs):
    inputs, (own_ref, cross_ref, small_ref), held = refs[:9], refs[9:12], refs[12:21]
    out_ref, sems = refs[21:]
    copies = [pltpu.make_async_copy(source, to, sems.at[at]) for at, (source, to) in enumerate(zip(inputs, held))]
    for copy in copies:
        copy.start()
    values_ref, source_ref, label_ref, lookup_ref, velocity_ref, heat_ref, rate_ref, polar_ref, azimuth_ref = held
    planes, rows, _ = values_ref.shape
    part = rows * planes // 8
    lane = lanes((8, 128))
    copies[3].wait()
    found = jnp.zeros((8, 128), jnp.int32)
    for at in range(lookup_ref.shape[0]):
        found = jnp.where(lane == 3 * part * REACH_COLUMNS + at, lookup_ref[at] + 1, found)
    extras = [found.astype(jnp.float32)] * 2
    for which, ref in enumerate((values_ref, source_ref, label_ref)):
        copies[which].wait()
        for plane in range(planes):
            for row in range(rows):
                at, sub = divmod(row * planes + plane, 8)
                value = ref[plane, row : row + 1, :]
                if which == 2:
                    value = (value + 1).astype(jnp.float32)
                out_ref[which * part + at, sub : sub + 1, :] = value
    left = lax.axis_index("modes") < lax.axis_size("modes") // 2
    for at in range(3 * part):
        sides = out_ref[at, :, 0:128], out_ref[at, :, 128:256]
        own_ref[at] = jnp.where(left, sides[0], sides[1])
        cross_ref[at] = jnp.where(left, sides[1], sides[0])
        place = at * REACH_COLUMNS
        here = (lane >= place) & (lane < place + REACH_COLUMNS)
        extras[0] = jnp.where(here, pltpu.roll(sides[1], place, axis=1), extras[0])
        extras[1] = jnp.where(here, pltpu.roll(sides[0], (place + REACH_COLUMNS) % 128, axis=1), extras[1])
    own_ref[3 * part] = jnp.where(left, extras[0], extras[1])
    cross_ref[3 * part] = jnp.where(left, extras[1], extras[0])
    small_ref[...] = jnp.zeros(small_ref.shape, jnp.float32)
    for copy in copies[4:]:
        copy.wait()
    size, half_dir = velocity_ref.shape[0], polar_ref.shape[0]
    small_ref[0, 0:size] = velocity_ref[...]
    small_ref[1, 0:size] = heat_ref[...]
    small_ref[2:5, 0:size] = rate_ref[...]
    for start in range(0, 128, PART):
        small_ref[8, start : start + half_dir] = polar_ref[...]
        small_ref[9, start : start + half_dir] = azimuth_ref[...]


def table_kernel(parts, per_part, half_dir, *refs):
    lookups = refs[:-4]
    small_ref, out_ref, work_ref, axes_ref = refs[-4:]
    padded = -(-per_part // 8) * 8
    lane = lanes((1, 128))

    last = lookups[0].shape[0] - 1
    modes = lax.axis_index("modes")
    found = jnp.zeros((1, 128), jnp.float32)
    owner = jnp.zeros((1, 128), jnp.int32)
    for part, ref in enumerate(lookups):
        place = last * REACH_COLUMNS
        row = jnp.where((lane >= place) & (lane < place + per_part), ref[last, 0:1, :], 0.0)
        found = found + pltpu.roll(row, (part * PART - place) % 128, axis=1)
        owner = jnp.where(lane // PART == part, modes ^ part, owner)
    index = found.astype(jnp.int32) - 1
    valid = index >= 0
    index = jnp.broadcast_to(jnp.where(valid, index, 0), (8, 128))
    picked = jnp.take_along_axis(small_ref[0:8, :], index, axis=1, mode="promise_in_bounds")
    frequency = owner * per_part + lane % PART
    spectral = (frequency.astype(jnp.float32) + 1.0) / (parts * per_part)
    velocity = jnp.where(valid, picked[0:1], 1.0)
    capacity = jnp.where(valid, picked[1:2] * spectral, 0.0)
    rates = [jnp.where(valid, picked[2 + k : 3 + k], 1.0) for k in range(3)]

    conducts, inverses = [], []
    for k in range(3):
        rate_total = jnp.sum(capacity * rates[k], axis=1, keepdims=True)
        cond_total = jnp.sum(capacity * velocity * velocity / (3.0 * rates[k]), axis=1, keepdims=True)
        conducts.append(cond_total / rate_total)
        inverses.append(1.0 / (2 * half_dir * rate_total))
    sub = sublanes((8, 128))

    def by_label(values):
        found = jnp.zeros((8, 128), jnp.float32)
        for code, value in zip(CODES, values):
            found = jnp.where(sub == code, value, found)
        return found

    out_ref[TABLE_AT["inverse_rate",]] = by_label(inverses)
    out_ref[TABLE_AT["conduct",]] = by_label(conducts)
    top = 1.0 + 12.0 * jnp.maximum(jnp.maximum(conducts[0], conducts[1]), conducts[2])
    top = jnp.broadcast_to(top, (8, 128))
    theta = (top + 1.0) / 2.0
    delta = (top - 1.0) / 2.0
    sigma = theta / delta
    rho = 1.0 / sigma
    out_ref[TABLE_AT["inverse_theta",]] = 1.0 / theta
    for step in range(CHEB - 1):
        rho_new = 1.0 / (2.0 * sigma - rho)
        out_ref[TABLE_AT["keep", step]] = rho_new * rho
        out_ref[TABLE_AT["gain", step]] = 2.0 * rho_new / delta
        rho = rho_new

    angles = small_ref[8:16, :]
    cosines, sines = jnp.cos(angles), jnp.sin(angles)
    real = (lane % PART) < half_dir
    u = [cosines[0:1], sines[0:1] * cosines[1:2], sines[0:1] * sines[1:2]]
    u = [jnp.where(real, part, 0.0) for part in u]
    a = [jnp.abs(part) for part in u]
    total = a[0] + a[1] + a[2]
    sides = [jnp.where(part >= 0.0, 1.0, -1.0) for part in u]

    products = {(): jnp.where(real, 1.0, 0.0)}
    for degree in (1, 2, 3):
        for axes in itertools.combinations_with_replacement(range(3), degree):
            products[axes] = products[axes[:-1]] * a[axes[-1]]
    masks = {}
    for degree in range(4):
        for _, pattern in MONO[degree]:
            if pattern not in masks:
                same = flipped = jnp.ones((1, 128), jnp.float32)
                for axis, sign in pattern:
                    if axis == 0:
                        flipped = jnp.zeros((1, 128), jnp.float32)
                    else:
                        same = same * jnp.where(sides[axis] == -sign, 1.0, 0.0)
                        flipped = flipped * jnp.where(sides[axis] == sign, 1.0, 0.0)
                masks[pattern] = (same + flipped, same - flipped)
    axes_ref[...] = jnp.zeros(axes_ref.shape, jnp.float32)
    weights = {"u": None, "v": total}
    weights.update({axis: u[axis] * (1.0 / (2 * half_dir)) for axis in range(3)})
    for at, (kind, degree, (axes, pattern)) in enumerate(COLUMNS):
        even, odd = masks[pattern]
        row = products[axes] * (even if kind in ("u", "v") else odd)
        if weights[kind] is not None:
            row = row * weights[kind]
        axes_ref[at : at + 1, :] = row

    columns = jnp.concatenate([velocity, capacity] + rates + [jnp.zeros((3, 128), jnp.float32)], axis=0).T

    def spread(at):
        found = jnp.zeros((padded, 128), jnp.float32)
        where = lanes((padded, 128)) // PART
        for part in range(parts):
            column = columns[part * PART : part * PART + padded, at : at + 1]
            found = jnp.where(where == part, column, found)
        return found

    speed, stored = spread(0), spread(1)
    loss = [spread(2 + k) for k in range(3)]
    inverse = [1.0 / (speed * total + loss[k]) for k in range(3)]
    weight = [stored]
    for _ in range(4):
        weight.append(weight[-1] * speed)
    chains = {}
    for length in (1, 2, 3):
        for labels in itertools.combinations_with_replacement(range(3), length):
            chains[labels] = inverse[labels[0]] if length == 1 else chains[labels[:-1]] * inverse[labels[-1]]
    work_ref[...] = jnp.zeros(work_ref.shape, jnp.float32)
    for name, (power, rated, index) in GROUPS.items():
        for code, terms in index.items():
            field = sum(sign * chains[tuple(sorted(labels))] for sign, labels in terms) * weight[power]
            if rated:
                field = field * loss[terms[0][1][0]]
            at = GROUP_AT[name] * 8 + code
            work_ref[at : at + 1, :] = jnp.sum(field, axis=0, keepdims=True)
    sums = lax.dot_general(
        work_ref[...],
        axes_ref[...],
        (((1,), (1,)), ((), ())),
        precision=HIGHEST,
        preferred_element_type=jnp.float32,
    )
    for at, key in enumerate(TABLES):
        if len(key) == 4:
            row, column = GROUP_AT[key[0]] * 8, COLUMN_AT[key[1:]]
            values = sums[row : row + 8, column : column + 1]
            if key[0] in ("u3", "u2"):
                row, column = GROUP_AT["x" + key[0][1]] * 8, COLUMN_AT[("v",) + key[2:]]
                values = values + sums[row : row + 8, column : column + 1]
            out_ref[at] = jnp.broadcast_to(values, (8, 128))


SIGNED = [(axis, sign) for axis in range(3) for sign in (-1, 1)]


def follows(earlier, step):
    return all((step[0], -step[1]) != before for before in earlier)


def displacement(steps):
    found = [0, 0, 0]
    for axis, sign in steps:
        found[axis] += sign
    return tuple(found)


def ends_of_two():
    found = {}
    for first in SIGNED:
        for second in SIGNED:
            if follows((first,), second):
                found.setdefault(tuple(sorted((first, second))), []).append(first)
    return found


ENDS = ends_of_two()
REACH = SWEEPS
FAR = [(z, y) for z in range(-3, 4) for y in range(-3, 4) if abs(z) + abs(y) <= 3]
NEAR = [(z, y) for z in range(-2, 3) for y in range(-2, 3) if abs(z) + abs(y) <= 2]
FAR_AT = {key: at for at, key in enumerate(FAR)}
NEAR_AT = {key: at for at, key in enumerate(NEAR)}


def pick(table, index):
    return jnp.take_along_axis(table, index, axis=0, mode="promise_in_bounds")


class Cells:
    def __init__(self, entry, far_ref, source_ref, code_ref):
        self.entry = entry
        self.refs = (far_ref, source_ref, code_ref)
        self.known = {}

    def get(self, which, place):
        key = (which, place)
        if key not in self.known:
            x, y, z = place
            at = FAR_AT[z, y] if which == 0 else NEAR_AT[z, y]
            self.known[key] = self.refs[which][at, self.entry + REACH + x]
        return self.known[key]

    def code(self):
        if "alike" not in self.known:
            code = self.get(2, (0, 0, 0))
            expected = jnp.where(code == CODES[0], -1, 2 * code)
            self.known["alike"] = (expected, jnp.where(code == CODES[1], ALIKE[1], ALIKE[2]))
        return self.known["alike"]

    def rise(self, place, step):
        further = list(place)
        further[step[0]] += step[1]
        return self.get(0, tuple(further)) - self.get(0, place)


class Packed(Cells):
    def __init__(self, entry, upper, planes, raw, middle, far_ref, source_ref, code_ref):
        super().__init__(entry, far_ref, source_ref, code_ref)
        self.upper, self.planes, self.raw, self.middle = upper, planes, raw, middle

    def get(self, which, place):
        key = (which, place)
        if key not in self.known:
            x, y, z = place
            at = FAR_AT[z, y] if which == 0 else NEAR_AT[z, y]
            ref = self.refs[which]
            found = []
            for row in range(2):
                entry = self.entry + (REACH + x + row)
                straight = ref[at, entry + 2 * self.upper]
                turned = ref[at, entry + 2 * (1 - self.upper)]
                found.append(jnp.where(self.raw, straight, pltpu.roll(turned, self.planes, axis=0)))
            self.known[key] = jnp.where(self.middle, found[0], pltpu.roll(found[1], 64, axis=1))
        return self.known[key]


def alike(pair, code):
    expected, place = code
    return jnp.where(pair == expected, place, pair)


class Sums:
    def __init__(self, count=4):
        self.parts = [None] * count
        self.at = 0

    def add(self, value):
        held = self.parts[self.at]
        self.parts[self.at] = value if held is None else held + value
        self.at = (self.at + 1) % len(self.parts)

    def total(self):
        held = [part for part in self.parts if part is not None]
        while len(held) > 1:
            held = [sum(held[at + 1 : at + 2], held[at]) for at in range(0, len(held), 2)]
        return held[0]


def energy_of(cells_list, table):
    sums = [Sums() for _ in cells_list]
    here = (0, 0, 0)
    codes = [cells.get(2, here) for cells in cells_list]
    rest = table(("u0", "u", 0, MONO[0][0]))
    for cells, code, held in zip(cells_list, codes, sums):
        held.add(pick(rest, code) * cells.get(1, here))
    for step in SIGNED:
        mono, _ = canonical((step,))
        rest = table(("u0d", "u", 1, mono))
        for cells, code, held in zip(cells_list, codes, sums):
            held.add(pick(rest, code) * cells.rise(here, step))
    two = {}
    for first in SIGNED:
        place = displacement((first,))
        mono, _ = canonical((first,))
        nears = [cells.get(2, place) for cells in cells_list]
        two[first] = pairs = [near + code for near, code in zip(nears, codes)]
        one, other = table(("u1", "u", 1, mono)), table(("v1", "v", 1, mono))
        for cells, near, pair, held in zip(cells_list, nears, pairs, sums):
            held.add((pick(one, near) - pick(other, pair)) * cells.get(1, place))
        for step in SIGNED:
            if follows((first,), step):
                mono, _ = canonical((first, step))
                one, other = table(("u1d", "u", 2, mono)), table(("v1d", "v", 2, mono))
                for cells, near, pair, held in zip(cells_list, nears, pairs, sums):
                    held.add((pick(one, near) - pick(other, pair)) * cells.rise(place, step))
    for steps, firsts in ENDS.items():
        place = displacement(steps)
        index = []
        for at, cells in enumerate(cells_list):
            end = cells.get(2, place)
            mine = []
            for first in firsts:
                pair = cells.get(2, displacement((first,))) + end
                mine.append((alike(pair, cells.code()), (pair + codes[at]) & 7))
            index.append(mine)
        cases = [(None, "2", canonical(steps)[0], 2)]
        cases += [(step, "3", canonical(steps + (step,))[0], 3) for step in SIGNED if follows(steps, step)]
        for step, which, mono, degree in cases:
            one, other = table(("u" + which, "u", degree, mono)), table(("a" + which, "v", degree, mono))
            for cells, mine, held in zip(cells_list, index, sums):
                factor = None
                for pair, triple in mine:
                    term = pick(one, pair) - pick(other, triple)
                    factor = term if factor is None else factor + term
                held.add(factor * (cells.get(1, place) if step is None else cells.rise(place, step)))
    return [held.total() for held in sums]


def flux_of(cells, table):
    sums = [Sums(2) for _ in range(3)]
    here = (0, 0, 0)
    code = cells.get(2, here)

    def signed(value, side):
        return value if side > 0 else -value

    for step in SIGNED:
        mono, side = canonical((step,))
        rise = signed(cells.rise(here, step), side)
        for axis in range(3):
            sums[axis].add(pick(table(("f0d", axis, 1, mono)), code) * rise)
    for first in SIGNED:
        place = displacement((first,))
        pair = cells.get(2, place) + code
        mono, side = canonical((first,))
        value = signed(cells.get(1, place), side)
        for axis in range(3):
            sums[axis].add(pick(table(("v1", axis, 1, mono)), pair) * value)
        for step in SIGNED:
            if follows((first,), step):
                mono, side = canonical((first, step))
                value = signed(cells.rise(place, step), side)
                for axis in range(3):
                    sums[axis].add(pick(table(("v1d", axis, 2, mono)), pair) * value)
    for steps, firsts in ENDS.items():
        place = displacement(steps)
        end = cells.get(2, place)
        index = []
        for first in firsts:
            pair = cells.get(2, displacement((first,))) + end
            index.append((alike(pair, cells.code()), (pair + code) & 7))
        cases = [(None, "2", canonical(steps), 2)]
        cases += [(step, "3", canonical(steps + (step,)), 3) for step in SIGNED if follows(steps, step)]
        for step, which, (mono, side), degree in cases:
            value = signed(cells.get(1, place) if step is None else cells.rise(place, step), side)
            for axis in range(3):
                one, other = table(("a" + which, axis, degree, mono)), table(("x" + which, axis, degree, mono))
                factor = None
                for pair, triple in index:
                    term = pick(one, triple) - pick(other, pair)
                    factor = term if factor is None else factor + term
                sums[axis].add(factor * value)
    return [held.total() for held in sums]


def main_kernel(groups, places, *refs):
    blocks = refs[: 2 * groups]
    table_ref, temperature_ref, flux_ref, base_ref, source_base_ref, code_base_ref = refs[2 * groups : 2 * groups + 6]
    far_ref, near_ref, code_ref, kappa_ref, force_ref, coef_ref, mismatch_ref, first_ref, second_ref = refs[
        2 * groups + 6 :
    ]
    planes, rows, tile = temperature_ref.shape
    width = tile * lax.axis_size("modes")
    parts = rows * planes // 8
    length = groups * rows
    lane, sub = lanes((8, 128)), sublanes((8, 128))
    lower = sub < planes
    plane = sub % planes
    modes = lax.axis_index("modes")
    leads, swaps, others, core_first, own_lead, own_upper = places()

    margin = (128 - tile) // 2
    start = modes * tile - margin
    column = start + lane
    chip = modes // 2
    inside = (column >= jnp.maximum(chip * 128 - REACH_COLUMNS, 0)) & (
        column < jnp.minimum(chip * 128 + 128 + REACH_COLUMNS, width)
    )
    left = (start + 128) // 128 - 1
    turn = 128 - (start - left * 128)
    from_main = jnp.where(lane >= 128 - turn, left, left + 1) == chip

    def window(main, extra, at):
        away = jnp.where(chip == 0, 0, 128 - REACH_COLUMNS) - at * REACH_COLUMNS
        extra = pltpu.roll(extra, lax.rem(away + 128, 128), axis=1)
        return pltpu.roll(jnp.where(from_main, main, extra), turn, axis=1)

    def paired_rows(first, second, swap):
        low, high = jnp.where(swap, second, first), jnp.where(swap, first, second)
        return (
            jnp.where(lower, low, pltpu.roll(high, planes, axis=0)),
            jnp.where(lower, pltpu.roll(low, planes, axis=0), high),
        )

    for group in range(groups):
        one, (two, other) = blocks[group], [blocks[groups + at] for at in others[group]]
        swap = swaps[group]

        def both(at):
            second = two[at] if other is two else jnp.where(core_first, two[at], other[at])
            return paired_rows(one[at], second, swap)

        extra = both(3 * parts)
        for which, ref in enumerate((base_ref, source_base_ref, code_base_ref)):
            for part in range(parts):
                place = which * parts + part
                pair = [window(main, more, place) for main, more in zip(both(place), extra)]
                for row in range(2):
                    at = REACH + leads[group] + 2 * part + row
                    if which < 2:
                        ref[at] = jnp.where(inside, pair[row], 0.0)
                    else:
                        ref[at] = jnp.where(inside, pair[row], 0.0).astype(jnp.int32)

    for ref in (base_ref, source_base_ref, code_base_ref):
        none = jnp.zeros((8, 128), ref.dtype)
        for at in range(REACH):
            ref[at] = jnp.where(lower, none, pltpu.roll(ref[at + length], planes, axis=0))
            ref[length + REACH + at] = jnp.where(lower, pltpu.roll(ref[REACH + at], planes, axis=0), none)

    conduct = table_ref[TABLE_AT["conduct",]]

    def shift_plane(value, z, none):
        if z == 0:
            return value
        return jnp.where((plane + z >= 0) & (plane + z < planes), pltpu.roll(value, (-z) % 8, axis=0), none)

    def spread(reach, value, out, keys, at, masked):
        beyond = max(REACH - at, at - (REACH + length - 1), 0)
        for y in sorted({y for _, y in keys}):
            if abs(y) + beyond > reach:
                continue
            moved = pltpu.roll(value, (-y) % 128, axis=1) if y else value
            for z in sorted({z for z, other in keys if other == y}):
                if abs(y) + abs(z) + beyond > reach:
                    continue
                if masked:
                    out[keys[z, y], at] = shift_plane(moved, z, 0.0)
                else:
                    out[keys[z, y], at] = pltpu.roll(moved, (-z) % 8, axis=0) if z else moved

    for at in range(length + 2 * REACH):
        spread(3, base_ref[at], far_ref, FAR_AT, at, True)
        spread(2, source_base_ref[at], near_ref, NEAR_AT, at, True)
        label = code_base_ref[at]
        kind = jnp.maximum(label - 1, 0)
        code = jnp.where(kind == 2, CODES[2], kind)
        kappa_ref[at] = jnp.where(label > 0, pick(conduct, code), 0.0)
        spread(2, code, code_ref, NEAR_AT, at, False)

    def table(key):
        return table_ref[TABLE_AT[key]]

    def forcing(step, _):
        entries = (2 * step, 2 * step + 1)
        cells_list = [Cells(entry, far_ref, near_ref, code_ref) for entry in entries]
        energies = energy_of(cells_list, table)
        scale = table_ref[TABLE_AT["inverse_rate",]]
        for entry, cells, energy in zip(entries, cells_list, energies):
            force = energy * pick(scale, cells.get(2, (0, 0, 0)))
            force_ref[entry] = jnp.where(code_base_ref[entry + REACH] > 0, force, 0.0)
        return 0

    lax.fori_loop(0, length // 2, forcing, 0)

    none = jnp.zeros((8, 128), jnp.float32)
    inverse_theta = table_ref[TABLE_AT["inverse_theta",]]
    for entry in range(length):
        kappa = kappa_ref[entry + REACH]
        real = code_base_ref[entry + REACH] > 0
        others = [
            kappa_ref[entry + REACH - 1],
            kappa_ref[entry + REACH + 1],
            pltpu.roll(kappa, 1, axis=1),
            pltpu.roll(kappa, 127, axis=1),
            shift_plane(kappa, -1, 0.0),
            shift_plane(kappa, 1, 0.0),
        ]
        faces = [jnp.where(real, 0.5 * (kappa + other), 0.0) for other in others]
        coef_ref[6, entry] = 1.0 + ((faces[0] + faces[1]) + (faces[2] + faces[3]) + (faces[4] + faces[5]))
        faces[4] = jnp.where(plane >= 1, faces[4], 0.0)
        faces[5] = jnp.where(plane < planes - 1, faces[5], 0.0)
        for at in range(6):
            coef_ref[at, entry] = faces[at]
        mismatch_ref[entry] = force_ref[entry]
        first_ref[entry + 1] = force_ref[entry] * inverse_theta

    def edges(ref):
        ref[0] = jnp.where(lower, none, pltpu.roll(ref[length], planes, axis=0))
        ref[length + 1] = jnp.where(lower, pltpu.roll(ref[1], planes, axis=0), none)

    edges(first_ref)
    correction = [first_ref[own_lead + row + 1] for row in range(rows)]
    for step in range(CHEB - 1):
        old_ref, new_ref = (first_ref, second_ref) if step % 2 == 0 else (second_ref, first_ref)
        keep = table_ref[TABLE_AT["keep", step]]
        gain = table_ref[TABLE_AT["gain", step]]
        for entry in range(length):
            value = old_ref[entry + 1]
            flow = coef_ref[6, entry] * value - coef_ref[0, entry] * old_ref[entry]
            flow = flow - coef_ref[1, entry] * old_ref[entry + 2]
            side = coef_ref[2, entry] * pltpu.roll(value, 1, axis=1)
            side = side + coef_ref[3, entry] * pltpu.roll(value, 127, axis=1)
            deep = coef_ref[4, entry] * pltpu.roll(value, 1, axis=0)
            deep = deep + coef_ref[5, entry] * pltpu.roll(value, 7, axis=0)
            mismatch = mismatch_ref[entry] - (flow - (side + deep))
            if step < CHEB - 2:
                mismatch_ref[entry] = mismatch
            new_ref[entry + 1] = keep * value + gain * mismatch
        if step < CHEB - 2:
            edges(new_ref)
        correction = [held + new_ref[own_lead + row + 1] for row, held in enumerate(correction)]

    def cut(value):
        value = jnp.where(own_upper, pltpu.roll(value, planes, axis=0), value)
        return pltpu.roll(value, 128 - margin, axis=1)[0:planes, 0:tile]

    for row in range(rows):
        entry = own_lead + row
        found = cut(base_ref[entry + REACH] + force_ref[entry] + correction[row])
        for at in range(planes):
            temperature_ref[at, row : row + 1, :] = found[at : at + 1]

    upper = jnp.where(own_upper, 1, 0)
    raw = jnp.where(lower, 0, 1) == upper
    middle = (lane >= margin) & (lane < margin + tile)
    cells = Packed(own_lead, upper, planes, raw, middle, far_ref, near_ref, code_ref)
    for axis, found in enumerate(flux_of(cells, table)):
        for row in range(2):
            turned = pltpu.roll(found, 128 - margin - row * tile, axis=1)[:, 0:tile]
            for half in range(2):
                for at in range(planes):
                    line, place = half * planes + at, row + 2 * half
                    flux_ref[axis, at, place : place + 1, :] = turned[line : line + 1]


def on_device(
    thermal_deviation_iterate,
    volumetric_source_term,
    node_substance_label,
    spectral_table_lookup,
    propagation_velocity_table,
    specific_heat_table,
    collision_frequency_table,
    ordinate_inclination,
    ordinate_longitude,
):
    planes, rows, width = thermal_deviation_iterate.shape
    modes, space = lax.axis_size("modes"), lax.axis_size("space")
    tile = width // modes
    per_part = spectral_table_lookup.shape[0]
    half_dir = ordinate_inclination.shape[0]
    assert planes == 4 and rows == 4 and width == 256
    assert modes == 4 and per_part <= PART and half_dir <= PART
    halo = -(-REACH_COLUMNS // rows)
    assert tile * 2 == 128 and 3 * rows * planes // 8 * REACH_COLUMNS + per_part <= 128
    vmem = pl.BlockSpec(memory_space=pltpu.VMEM)
    parts = rows * planes // 8
    depth = 3 * parts + 1
    arguments = (
        thermal_deviation_iterate,
        volumetric_source_term,
        node_substance_label,
        spectral_table_lookup,
        propagation_velocity_table,
        specific_heat_table,
        collision_frequency_table.T,
        ordinate_inclination,
        ordinate_longitude,
    )
    held = [(pltpu.SMEM if at == 3 else pltpu.VMEM)(x.shape, x.dtype) for at, x in enumerate(arguments)]
    part_shape = pltpu.VMEM((depth, 8, 128), jnp.float32)
    payload, crossing, small = pl.pallas_call(
        pack_kernel,
        out_shape=(part_shape, part_shape, pltpu.VMEM((16, 128), jnp.float32)),
        in_specs=[pl.BlockSpec(memory_space=pltpu.HBM)] * len(arguments),
        out_specs=(vmem, vmem, vmem),
        scratch_shapes=held + [pltpu.VMEM((depth - 1, 8, width), jnp.float32), pltpu.SemaphoreType.DMA((len(arguments),))],
        name="pack",
    )(*arguments)

    if space == 8:
        groups = 4
        fetched = []
        for apart, across in zip((*zip(*APART), (APART_BOTH,) * 2), (1, 2, 3, 0)):
            moves = []
            for m in range(modes):
                for s in range(space):
                    source = s ^ apart[m % 2]
                    if abs(source - s) > halo:
                        source = s
                    moves.append(((m ^ across) * space + source, m * space + s))
            fetched.append(lax.ppermute(crossing if across >= 2 else payload, ("modes", "space"), moves))
        swapped = [lax.ppermute(block, "modes", [(m, m ^ 1) for m in range(modes)]) for block in fetched[:3]]
        blocks = [payload] + fetched + swapped
        lookups = [payload] + fetched[:3]

        def places():
            m, s = lax.axis_index("modes"), lax.axis_index("space")
            core = lax.rem(m, 2)
            firsts = [(0,) + APART[c] for c in range(2)]
            seconds = [(APART_BOTH,) + APART[1 - c] for c in range(2)]
            leads, swaps, others = [], [], []
            for step in range(groups):
                owner = s ^ jnp.where(core == 0, firsts[0][step], firsts[1][step])
                leads.append(lax.rem(owner, groups) * rows)
                swaps.append(owner >= groups)
                others.append([seconds[c].index(firsts[c][step] ^ groups) for c in range(2)])
            return leads, swaps, others, core == 0, lax.rem(s, groups) * rows, s >= groups

    else:
        groups = halo + 1
        everything = lax.all_gather(payload, "space", axis=0, tiled=False)
        everything = jnp.pad(everything, ((halo, halo + 1), (0, 0), (0, 0), (0, 0)))
        first = lax.axis_index("space")
        near = lax.dynamic_slice_in_dim(everything, first, 2 * groups, 0)
        blocks = [near[at] for at in range(2 * groups)]
        lookups = [payload]
        for apart in range(1, modes):
            lookups.append(lax.ppermute(payload, "modes", [(m, m ^ apart) for m in range(modes)]))

        def places():
            same = [[step, step] for step in range(groups)]
            return [step * rows for step in range(groups)], [False] * groups, same, True, halo * rows, False

    tables = pl.pallas_call(
        lambda *refs: table_kernel(modes, per_part, half_dir, *refs),
        out_shape=pltpu.VMEM((len(TABLES), 8, 128), jnp.float32),
        in_specs=[vmem] * (len(lookups) + 1),
        out_specs=vmem,
        compiler_params=pltpu.CompilerParams(vmem_limit_bytes=8 * 1024 * 1024),
        scratch_shapes=[
            pltpu.VMEM((8 * len(GROUPS), 128), jnp.float32),
            pltpu.VMEM((128 * COLUMN_TILES, 128), jnp.float32),
        ],
        name="tables",
    )(
        *lookups,
        small,
    )
    length = groups * rows
    whole = length + 2 * REACH
    return pl.pallas_call(
        lambda *refs: main_kernel(groups, places, *refs),
        out_shape=(
            jax.ShapeDtypeStruct((planes, rows, tile), jnp.float32),
            jax.ShapeDtypeStruct((3, planes, rows, tile), jnp.float32),
        ),
        in_specs=[vmem] * (2 * groups + 1),
        out_specs=(vmem, vmem),
        scratch_shapes=[
            pltpu.VMEM((whole, 8, 128), jnp.float32),
            pltpu.VMEM((whole, 8, 128), jnp.float32),
            pltpu.VMEM((whole, 8, 128), jnp.int32),
            pltpu.VMEM((len(FAR), whole, 8, 128), jnp.float32),
            pltpu.VMEM((len(NEAR), whole, 8, 128), jnp.float32),
            pltpu.VMEM((len(NEAR), whole, 8, 128), jnp.int32),
            pltpu.VMEM((whole, 8, 128), jnp.float32),
            pltpu.VMEM((length, 8, 128), jnp.float32),
            pltpu.VMEM((7, length, 8, 128), jnp.float32),
            pltpu.VMEM((length, 8, 128), jnp.float32),
            pltpu.VMEM((length + 2, 8, 128), jnp.float32),
            pltpu.VMEM((length + 2, 8, 128), jnp.float32),
        ],
        compiler_params=pltpu.CompilerParams(vmem_limit_bytes=32 * 1024 * 1024),
        name="solve",
    )(*blocks, tables)


def solution(mesh):
    placed = (
        P(None, "space", None),
        P(None, "space", None),
        P(None, "space", None),
        P("modes"),
        P(),
        P(),
        P(),
        P(),
        P(),
    )
    return jax.shard_map(
        on_device,
        mesh=mesh,
        in_specs=placed,
        out_specs=(P(None, "space", "modes"), P(None, None, "space", "modes")),
        check_vma=False,
    )
```

```python
import itertools

import jax
import jax.numpy as jnp
from jax import lax
from jax.experimental import pallas as pl
from jax.experimental.pallas import tpu as pltpu
from jax.sharding import PartitionSpec as P


SWEEPS = 3
CHEB = 16
REACH_COLUMNS = SWEEPS + CHEB - 1
PART = 32
CODES = (0, 1, 3)
HIGHEST = lax.Precision.HIGHEST
APART = ((6, 2, 5), (7, 1, 4))
APART_BOTH = 3
ACROSS = (2, 3, 1, 0)


def monomials(degree):
    found = []
    for axes in itertools.combinations_with_replacement(range(3), degree):
        distinct = sorted(set(axes))
        for rest in itertools.product((-1, 1), repeat=max(len(distinct) - 1, 0)):
            found.append((axes, tuple(zip(distinct, (-1,) + rest)) if distinct else ()))
    return found


MONO = {degree: monomials(degree) for degree in range(4)}


def canonical(steps):
    axes = tuple(sorted(axis for axis, _ in steps))
    signs = dict(steps)
    first = signs[axes[0]]
    pattern = tuple((axis, signs[axis] * -first) for axis in sorted(signs))
    return (axes, pattern), -first


PAIRS = {CODES[a] + CODES[b]: [(1, (a, b))] for a, b in itertools.combinations_with_replacement(range(3), 2)}
TRIPLES = {
    CODES[a] + CODES[b] + CODES[c]: [(1, (a, b, c))]
    for a, b, c in itertools.combinations_with_replacement(range(3), 3)
    if (a, b, c) not in ((1, 1, 1), (2, 2, 2))
}
SINGLES = {CODES[a]: [(1, (a,))] for a in range(3)}
ALIKE = {1: 5, 2: 7}
PAIRS_ALIKE = dict(PAIRS)
EXTRA = {}
for label, place in ALIKE.items():
    PAIRS_ALIKE[place] = [(1, (label, label))]
    EXTRA[place] = [(-1, (label,) * 3)] + TRIPLES[(3 * CODES[label]) & 7]
GROUPS = {
    "u3": (3, False, PAIRS_ALIKE),
    "u2": (2, False, PAIRS_ALIKE),
    "u1d": (2, False, SINGLES),
    "u1": (1, False, SINGLES),
    "u0d": (1, True, SINGLES),
    "u0": (0, True, SINGLES),
    "a3": (4, False, TRIPLES),
    "x3": (4, False, EXTRA),
    "a2": (3, False, TRIPLES),
    "x2": (3, False, EXTRA),
    "v1d": (3, False, PAIRS),
    "v1": (2, False, PAIRS),
    "f0d": (2, False, SINGLES),
}
GROUP_AT = {name: at for at, name in enumerate(GROUPS)}
COLUMNS = (
    [("u", degree, mono) for degree in (3, 2, 1, 0) for mono in MONO[degree]]
    + [("v", degree, mono) for degree in (3, 2, 1) for mono in MONO[degree]]
    + [(axis, degree, mono) for axis in range(3) for degree in (3, 2, 1) for mono in MONO[degree]]
)
COLUMN_AT = {column: at for at, column in enumerate(COLUMNS)}
COLUMN_TILES = -(-len(COLUMNS) // 128)


def table_list():
    found = [("inverse_rate",), ("conduct",), ("inverse_theta",)]
    found += [("keep", step) for step in range(CHEB - 1)] + [("gain", step) for step in range(CHEB - 1)]
    for group, degree in (("u3", 3), ("u2", 2), ("u1d", 2), ("u1", 1), ("u0d", 1), ("u0", 0)):
        found += [(group, "u", degree, mono) for mono in MONO[degree]]
    for kind in ("v", 0, 1, 2):
        for group, degree in (("a3", 3), ("x3", 3), ("a2", 2), ("x2", 2), ("v1d", 2), ("v1", 1)):
            if kind == "v" and group[0] == "x":
                continue
            found += [(group, kind, degree, mono) for mono in MONO[degree]]
    for kind in (0, 1, 2):
        found += [("f0d", kind, 1, mono) for mono in MONO[1]]
    return found


TABLES = table_list()
TABLE_AT = {key: at for at, key in enumerate(TABLES)}


def lanes(shape):
    return lax.broadcasted_iota(jnp.int32, shape, len(shape) - 1)


def sublanes(shape):
    return lax.broadcasted_iota(jnp.int32, shape, len(shape) - 2)


def pack_kernel(*refs):
    inputs, (own_ref, cross_ref, small_ref), held = refs[:9], refs[9:12], refs[12:21]
    out_ref, sems = refs[21:]
    copies = [pltpu.make_async_copy(source, to, sems.at[at]) for at, (source, to) in enumerate(zip(inputs, held))]
    for copy in copies:
        copy.start()
    values_ref, source_ref, label_ref, lookup_ref, velocity_ref, heat_ref, rate_ref, polar_ref, azimuth_ref = held
    planes, rows, _ = values_ref.shape
    part = rows * planes // 8
    lane = lanes((8, 128))
    copies[3].wait()
    found = jnp.zeros((8, 128), jnp.int32)
    for at in range(lookup_ref.shape[0]):
        found = jnp.where(lane == 3 * part * REACH_COLUMNS + at, lookup_ref[at] + 1, found)
    extras = [found.astype(jnp.float32)] * 2
    for which, ref in enumerate((values_ref, source_ref, label_ref)):
        copies[which].wait()
        for plane in range(planes):
            for row in range(rows):
                at, sub = divmod(row * planes + plane, 8)
                value = ref[plane, row : row + 1, :]
                if which == 2:
                    value = (value + 1).astype(jnp.float32)
                out_ref[which * part + at, sub : sub + 1, :] = value
    left = lax.axis_index("modes") < lax.axis_size("modes") // 2
    for at in range(3 * part):
        sides = out_ref[at, :, 0:128], out_ref[at, :, 128:256]
        own_ref[at] = jnp.where(left, sides[0], sides[1])
        cross_ref[at] = jnp.where(left, sides[1], sides[0])
        place = at * REACH_COLUMNS
        here = (lane >= place) & (lane < place + REACH_COLUMNS)
        extras[0] = jnp.where(here, pltpu.roll(sides[1], place, axis=1), extras[0])
        extras[1] = jnp.where(here, pltpu.roll(sides[0], (place + REACH_COLUMNS) % 128, axis=1), extras[1])
    own_ref[3 * part] = jnp.where(left, extras[0], extras[1])
    cross_ref[3 * part] = jnp.where(left, extras[1], extras[0])
    small_ref[...] = jnp.zeros(small_ref.shape, jnp.float32)
    for copy in copies[4:]:
        copy.wait()
    size, half_dir = velocity_ref.shape[0], polar_ref.shape[0]
    small_ref[10:11, :] = found[0:1].astype(jnp.float32)
    small_ref[0, 0:size] = velocity_ref[...]
    small_ref[1, 0:size] = heat_ref[...]
    small_ref[2:5, 0:size] = rate_ref[...]
    for start in range(0, 128, PART):
        small_ref[8, start : start + half_dir] = polar_ref[...]
        small_ref[9, start : start + half_dir] = azimuth_ref[...]


def table_kernel(masks, per_part, half_dir, *refs):
    lookups = refs[:-4]
    small_ref, out_ref, work_ref, axes_ref = refs[-4:]
    parts = len(masks)
    padded = -(-per_part // 8) * 8
    lane = lanes((1, 128))

    last = lookups[0].shape[0] - 1
    rows = [small_ref[10:11, :]] + [ref[last, 0:1, :] for ref in lookups]
    modes = lax.axis_index("modes")
    found = jnp.zeros((1, 128), jnp.float32)
    owner = jnp.zeros((1, 128), jnp.int32)
    for part, row in zip(masks, rows):
        place = last * REACH_COLUMNS
        row = jnp.where((lane >= place) & (lane < place + per_part), row, 0.0)
        found = found + pltpu.roll(row, (part * PART - place) % 128, axis=1)
        owner = jnp.where(lane // PART == part, modes ^ part, owner)
    index = found.astype(jnp.int32) - 1
    valid = index >= 0
    index = jnp.broadcast_to(jnp.where(valid, index, 0), (8, 128))
    picked = jnp.take_along_axis(small_ref[0:8, :], index, axis=1, mode="promise_in_bounds")
    frequency = owner * per_part + lane % PART
    spectral = (frequency.astype(jnp.float32) + 1.0) / (parts * per_part)
    velocity = jnp.where(valid, picked[0:1], 1.0)
    capacity = jnp.where(valid, picked[1:2] * spectral, 0.0)
    rates = [jnp.where(valid, picked[2 + k : 3 + k], 1.0) for k in range(3)]

    conducts, inverses = [], []
    for k in range(3):
        rate_total = jnp.sum(capacity * rates[k], axis=1, keepdims=True)
        cond_total = jnp.sum(capacity * velocity * velocity / (3.0 * rates[k]), axis=1, keepdims=True)
        conducts.append(cond_total / rate_total)
        inverses.append(1.0 / (2 * half_dir * rate_total))
    sub = sublanes((8, 128))

    def by_label(values):
        found = jnp.zeros((8, 128), jnp.float32)
        for code, value in zip(CODES, values):
            found = jnp.where(sub == code, value, found)
        return found

    out_ref[TABLE_AT["inverse_rate",]] = by_label(inverses)
    out_ref[TABLE_AT["conduct",]] = by_label(conducts)
    top = 1.0 + 12.0 * jnp.maximum(jnp.maximum(conducts[0], conducts[1]), conducts[2])
    top = jnp.broadcast_to(top, (8, 128))
    theta = (top + 1.0) / 2.0
    delta = (top - 1.0) / 2.0
    sigma = theta / delta
    rho = 1.0 / sigma
    out_ref[TABLE_AT["inverse_theta",]] = 1.0 / theta
    for step in range(CHEB - 1):
        rho_new = 1.0 / (2.0 * sigma - rho)
        out_ref[TABLE_AT["keep", step]] = rho_new * rho
        out_ref[TABLE_AT["gain", step]] = 2.0 * rho_new / delta
        rho = rho_new

    angles = small_ref[8:16, :]
    cosines, sines = jnp.cos(angles), jnp.sin(angles)
    real = (lane % PART) < half_dir
    u = [cosines[0:1], sines[0:1] * cosines[1:2], sines[0:1] * sines[1:2]]
    u = [jnp.where(real, part, 0.0) for part in u]
    a = [jnp.abs(part) for part in u]
    total = a[0] + a[1] + a[2]
    sides = [jnp.where(part >= 0.0, 1.0, -1.0) for part in u]

    products = {(): jnp.where(real, 1.0, 0.0)}
    for degree in (1, 2, 3):
        for axes in itertools.combinations_with_replacement(range(3), degree):
            products[axes] = products[axes[:-1]] * a[axes[-1]]
    masks = {}
    for degree in range(4):
        for _, pattern in MONO[degree]:
            if pattern not in masks:
                same = flipped = jnp.ones((1, 128), jnp.float32)
                for axis, sign in pattern:
                    if axis == 0:
                        flipped = jnp.zeros((1, 128), jnp.float32)
                    else:
                        same = same * jnp.where(sides[axis] == -sign, 1.0, 0.0)
                        flipped = flipped * jnp.where(sides[axis] == sign, 1.0, 0.0)
                masks[pattern] = (same + flipped, same - flipped)
    axes_ref[...] = jnp.zeros(axes_ref.shape, jnp.float32)
    weights = {"u": None, "v": total}
    weights.update({axis: u[axis] * (1.0 / (2 * half_dir)) for axis in range(3)})
    for at, (kind, degree, (axes, pattern)) in enumerate(COLUMNS):
        even, odd = masks[pattern]
        row = products[axes] * (even if kind in ("u", "v") else odd)
        if weights[kind] is not None:
            row = row * weights[kind]
        axes_ref[at : at + 1, :] = row

    columns = jnp.concatenate([velocity, capacity] + rates + [jnp.zeros((3, 128), jnp.float32)], axis=0).T

    def spread(at):
        found = jnp.zeros((padded, 128), jnp.float32)
        where = lanes((padded, 128)) // PART
        for part in range(parts):
            column = columns[part * PART : part * PART + padded, at : at + 1]
            found = jnp.where(where == part, column, found)
        return found

    speed, stored = spread(0), spread(1)
    loss = [spread(2 + k) for k in range(3)]
    inverse = [1.0 / (speed * total + loss[k]) for k in range(3)]
    weight = [stored]
    for _ in range(4):
        weight.append(weight[-1] * speed)
    chains = {}
    for length in (1, 2, 3):
        for labels in itertools.combinations_with_replacement(range(3), length):
            chains[labels] = inverse[labels[0]] if length == 1 else chains[labels[:-1]] * inverse[labels[-1]]
    work_ref[...] = jnp.zeros(work_ref.shape, jnp.float32)
    for name, (power, rated, index) in GROUPS.items():
        for code, terms in index.items():
            field = sum(sign * chains[tuple(sorted(labels))] for sign, labels in terms) * weight[power]
            if rated:
                field = field * loss[terms[0][1][0]]
            at = GROUP_AT[name] * 8 + code
            work_ref[at : at + 1, :] = jnp.sum(field, axis=0, keepdims=True)
    sums = lax.dot_general(
        work_ref[...],
        axes_ref[...],
        (((1,), (1,)), ((), ())),
        precision=HIGHEST,
        preferred_element_type=jnp.float32,
    )
    for at, key in enumerate(TABLES):
        if len(key) == 4:
            row, column = GROUP_AT[key[0]] * 8, COLUMN_AT[key[1:]]
            values = sums[row : row + 8, column : column + 1]
            if key[0] in ("u3", "u2"):
                row, column = GROUP_AT["x" + key[0][1]] * 8, COLUMN_AT[("v",) + key[2:]]
                values = values + sums[row : row + 8, column : column + 1]
            out_ref[at] = jnp.broadcast_to(values, (8, 128))


SIGNED = [(axis, sign) for axis in range(3) for sign in (-1, 1)]


def follows(earlier, step):
    return all((step[0], -step[1]) != before for before in earlier)


def displacement(steps):
    found = [0, 0, 0]
    for axis, sign in steps:
        found[axis] += sign
    return tuple(found)


def ends_of_two():
    found = {}
    for first in SIGNED:
        for second in SIGNED:
            if follows((first,), second):
                found.setdefault(tuple(sorted((first, second))), []).append(first)
    return found


ENDS = ends_of_two()
REACH = SWEEPS
FAR = [(z, y) for z in range(-3, 4) for y in range(-3, 4) if abs(z) + abs(y) <= 3]
NEAR = [(z, y) for z in range(-2, 3) for y in range(-2, 3) if abs(z) + abs(y) <= 2]
FAR_AT = {key: at for at, key in enumerate(FAR)}
NEAR_AT = {key: at for at, key in enumerate(NEAR)}


def pick(table, index):
    return jnp.take_along_axis(table, index, axis=0, mode="promise_in_bounds")


class Cells:
    def __init__(self, entry, far_ref, source_ref, code_ref):
        self.entry = entry
        self.refs = (far_ref, source_ref, code_ref)
        self.known = {}

    def get(self, which, place):
        key = (which, place)
        if key not in self.known:
            x, y, z = place
            at = FAR_AT[z, y] if which == 0 else NEAR_AT[z, y]
            self.known[key] = self.refs[which][at, self.entry + REACH + x]
        return self.known[key]

    def code(self):
        if "alike" not in self.known:
            code = self.get(2, (0, 0, 0))
            expected = jnp.where(code == CODES[0], -1, 2 * code)
            self.known["alike"] = (expected, jnp.where(code == CODES[1], ALIKE[1], ALIKE[2]))
        return self.known["alike"]

    def rise(self, place, step):
        further = list(place)
        further[step[0]] += step[1]
        return self.get(0, tuple(further)) - self.get(0, place)


class Packed(Cells):
    def __init__(self, entry, upper, planes, raw, middle, far_ref, source_ref, code_ref):
        super().__init__(entry, far_ref, source_ref, code_ref)
        self.upper, self.planes, self.raw, self.middle = upper, planes, raw, middle

    def get(self, which, place):
        key = (which, place)
        if key not in self.known:
            x, y, z = place
            at = FAR_AT[z, y] if which == 0 else NEAR_AT[z, y]
            ref = self.refs[which]
            found = []
            for row in range(2):
                entry = self.entry + (REACH + x + row)
                straight = ref[at, entry + 2 * self.upper]
                turned = ref[at, entry + 2 * (1 - self.upper)]
                found.append(jnp.where(self.raw, straight, pltpu.roll(turned, self.planes, axis=0)))
            self.known[key] = jnp.where(self.middle, found[0], pltpu.roll(found[1], 64, axis=1))
        return self.known[key]


def alike(pair, code):
    expected, place = code
    return jnp.where(pair == expected, place, pair)


class Sums:
    def __init__(self, count=4):
        self.parts = [None] * count
        self.at = 0

    def add(self, value):
        held = self.parts[self.at]
        self.parts[self.at] = value if held is None else held + value
        self.at = (self.at + 1) % len(self.parts)

    def total(self):
        held = [part for part in self.parts if part is not None]
        while len(held) > 1:
            held = [sum(held[at + 1 : at + 2], held[at]) for at in range(0, len(held), 2)]
        return held[0]


def energy_of(cells_list, table):
    sums = [Sums() for _ in cells_list]
    here = (0, 0, 0)
    codes = [cells.get(2, here) for cells in cells_list]
    rest = table(("u0", "u", 0, MONO[0][0]))
    for cells, code, held in zip(cells_list, codes, sums):
        held.add(pick(rest, code) * cells.get(1, here))
    for step in SIGNED:
        mono, _ = canonical((step,))
        rest = table(("u0d", "u", 1, mono))
        for cells, code, held in zip(cells_list, codes, sums):
            held.add(pick(rest, code) * cells.rise(here, step))
    two = {}
    for first in SIGNED:
        place = displacement((first,))
        mono, _ = canonical((first,))
        nears = [cells.get(2, place) for cells in cells_list]
        two[first] = pairs = [near + code for near, code in zip(nears, codes)]
        one, other = table(("u1", "u", 1, mono)), table(("v1", "v", 1, mono))
        for cells, near, pair, held in zip(cells_list, nears, pairs, sums):
            held.add((pick(one, near) - pick(other, pair)) * cells.get(1, place))
        for step in SIGNED:
            if follows((first,), step):
                mono, _ = canonical((first, step))
                one, other = table(("u1d", "u", 2, mono)), table(("v1d", "v", 2, mono))
                for cells, near, pair, held in zip(cells_list, nears, pairs, sums):
                    held.add((pick(one, near) - pick(other, pair)) * cells.rise(place, step))
    for steps, firsts in ENDS.items():
        place = displacement(steps)
        index = []
        for at, cells in enumerate(cells_list):
            end = cells.get(2, place)
            mine = []
            for first in firsts:
                pair = cells.get(2, displacement((first,))) + end
                mine.append((alike(pair, cells.code()), (pair + codes[at]) & 7))
            index.append(mine)
        cases = [(None, "2", canonical(steps)[0], 2)]
        cases += [(step, "3", canonical(steps + (step,))[0], 3) for step in SIGNED if follows(steps, step)]
        for step, which, mono, degree in cases:
            one, other = table(("u" + which, "u", degree, mono)), table(("a" + which, "v", degree, mono))
            for cells, mine, held in zip(cells_list, index, sums):
                factor = None
                for pair, triple in mine:
                    term = pick(one, pair) - pick(other, triple)
                    factor = term if factor is None else factor + term
                held.add(factor * (cells.get(1, place) if step is None else cells.rise(place, step)))
    return [held.total() for held in sums]


def flux_of(cells, table):
    sums = [Sums(2) for _ in range(3)]
    here = (0, 0, 0)
    code = cells.get(2, here)

    def signed(value, side):
        return value if side > 0 else -value

    for step in SIGNED:
        mono, side = canonical((step,))
        rise = signed(cells.rise(here, step), side)
        for axis in range(3):
            sums[axis].add(pick(table(("f0d", axis, 1, mono)), code) * rise)
    for first in SIGNED:
        place = displacement((first,))
        pair = cells.get(2, place) + code
        mono, side = canonical((first,))
        value = signed(cells.get(1, place), side)
        for axis in range(3):
            sums[axis].add(pick(table(("v1", axis, 1, mono)), pair) * value)
        for step in SIGNED:
            if follows((first,), step):
                mono, side = canonical((first, step))
                value = signed(cells.rise(place, step), side)
                for axis in range(3):
                    sums[axis].add(pick(table(("v1d", axis, 2, mono)), pair) * value)
    for steps, firsts in ENDS.items():
        place = displacement(steps)
        end = cells.get(2, place)
        index = []
        for first in firsts:
            pair = cells.get(2, displacement((first,))) + end
            index.append((alike(pair, cells.code()), (pair + code) & 7))
        cases = [(None, "2", canonical(steps), 2)]
        cases += [(step, "3", canonical(steps + (step,)), 3) for step in SIGNED if follows(steps, step)]
        for step, which, (mono, side), degree in cases:
            value = signed(cells.get(1, place) if step is None else cells.rise(place, step), side)
            for axis in range(3):
                one, other = table(("a" + which, axis, degree, mono)), table(("x" + which, axis, degree, mono))
                factor = None
                for pair, triple in index:
                    term = pick(one, triple) - pick(other, pair)
                    factor = term if factor is None else factor + term
                sums[axis].add(factor * value)
    return [held.total() for held in sums]


def main_kernel(groups, places, *refs):
    blocks = refs[: 2 * groups]
    table_ref, temperature_ref, flux_ref, base_ref, source_base_ref, code_base_ref = refs[2 * groups : 2 * groups + 6]
    far_ref, near_ref, code_ref, kappa_ref, force_ref, coef_ref, mismatch_ref, first_ref, second_ref = refs[
        2 * groups + 6 :
    ]
    planes, rows, tile = temperature_ref.shape
    width = tile * lax.axis_size("modes")
    parts = rows * planes // 8
    length = groups * rows
    lane, sub = lanes((8, 128)), sublanes((8, 128))
    lower = sub < planes
    plane = sub % planes
    modes = lax.axis_index("modes")
    leads, swap, holders, core_first, own_lead, own_upper = places()

    margin = (128 - tile) // 2
    start = modes * tile - margin
    column = start + lane
    chip = modes // 2
    inside = (column >= jnp.maximum(chip * 128 - REACH_COLUMNS, 0)) & (
        column < jnp.minimum(chip * 128 + 128 + REACH_COLUMNS, width)
    )
    left = (start + 128) // 128 - 1
    turn = 128 - (start - left * 128)
    from_main = jnp.where(lane >= 128 - turn, left, left + 1) == chip

    def window(main, extra, at):
        away = jnp.where(chip == 0, 0, 128 - REACH_COLUMNS) - at * REACH_COLUMNS
        extra = pltpu.roll(extra, lax.rem(away + 128, 128), axis=1)
        return pltpu.roll(jnp.where(from_main, main, extra), turn, axis=1)

    def paired_rows(first, second):
        low, high = jnp.where(swap, second, first), jnp.where(swap, first, second)
        return (
            jnp.where(lower, low, pltpu.roll(high, planes, axis=0)),
            jnp.where(lower, pltpu.roll(low, planes, axis=0), high),
        )

    for group in range(groups):
        def block(holder, at):
            first, second = [blocks[held] for held in holder]
            return first[at] if first is second else jnp.where(core_first, first[at], second[at])

        def both(at):
            first, second = [block(holder, at) for holder in holders[group]]
            return paired_rows(first, second)

        extra = both(3 * parts)
        for which, ref in enumerate((base_ref, source_base_ref, code_base_ref)):
            for part in range(parts):
                place = which * parts + part
                pair = [window(main, more, place) for main, more in zip(both(place), extra)]
                for row in range(2):
                    at = REACH + leads[group] + 2 * part + row
                    if which < 2:
                        ref[at] = jnp.where(inside, pair[row], 0.0)
                    else:
                        ref[at] = jnp.where(inside, pair[row], 0.0).astype(jnp.int32)

    for ref in (base_ref, source_base_ref, code_base_ref):
        none = jnp.zeros((8, 128), ref.dtype)
        for at in range(REACH):
            ref[at] = jnp.where(lower, none, pltpu.roll(ref[at + length], planes, axis=0))
            ref[length + REACH + at] = jnp.where(lower, pltpu.roll(ref[REACH + at], planes, axis=0), none)

    conduct = table_ref[TABLE_AT["conduct",]]

    def shift_plane(value, z, none):
        if z == 0:
            return value
        return jnp.where((plane + z >= 0) & (plane + z < planes), pltpu.roll(value, (-z) % 8, axis=0), none)

    def spread(reach, value, out, keys, at, masked):
        beyond = max(REACH - at, at - (REACH + length - 1), 0)
        for y in sorted({y for _, y in keys}):
            if abs(y) + beyond > reach:
                continue
            moved = pltpu.roll(value, (-y) % 128, axis=1) if y else value
            for z in sorted({z for z, other in keys if other == y}):
                if abs(y) + abs(z) + beyond > reach:
                    continue
                if masked:
                    out[keys[z, y], at] = shift_plane(moved, z, 0.0)
                else:
                    out[keys[z, y], at] = pltpu.roll(moved, (-z) % 8, axis=0) if z else moved

    for at in range(length + 2 * REACH):
        spread(3, base_ref[at], far_ref, FAR_AT, at, True)
        spread(2, source_base_ref[at], near_ref, NEAR_AT, at, True)
        label = code_base_ref[at]
        kind = jnp.maximum(label - 1, 0)
        code = jnp.where(kind == 2, CODES[2], kind)
        kappa_ref[at] = jnp.where(label > 0, pick(conduct, code), 0.0)
        spread(2, code, code_ref, NEAR_AT, at, False)

    def table(key):
        return table_ref[TABLE_AT[key]]

    def forcing(step, _):
        entries = (2 * step, 2 * step + 1)
        cells_list = [Cells(entry, far_ref, near_ref, code_ref) for entry in entries]
        energies = energy_of(cells_list, table)
        scale = table_ref[TABLE_AT["inverse_rate",]]
        for entry, cells, energy in zip(entries, cells_list, energies):
            force = energy * pick(scale, cells.get(2, (0, 0, 0)))
            force_ref[entry] = jnp.where(code_base_ref[entry + REACH] > 0, force, 0.0)
        return 0

    lax.fori_loop(0, length // 2, forcing, 0)

    none = jnp.zeros((8, 128), jnp.float32)
    inverse_theta = table_ref[TABLE_AT["inverse_theta",]]
    for entry in range(length):
        kappa = kappa_ref[entry + REACH]
        real = code_base_ref[entry + REACH] > 0
        others = [
            kappa_ref[entry + REACH - 1],
            kappa_ref[entry + REACH + 1],
            pltpu.roll(kappa, 1, axis=1),
            pltpu.roll(kappa, 127, axis=1),
            shift_plane(kappa, -1, 0.0),
            shift_plane(kappa, 1, 0.0),
        ]
        faces = [jnp.where(real, 0.5 * (kappa + other), 0.0) for other in others]
        coef_ref[6, entry] = 1.0 + ((faces[0] + faces[1]) + (faces[2] + faces[3]) + (faces[4] + faces[5]))
        faces[4] = jnp.where(plane >= 1, faces[4], 0.0)
        faces[5] = jnp.where(plane < planes - 1, faces[5], 0.0)
        for at in range(6):
            coef_ref[at, entry] = faces[at]
        mismatch_ref[entry] = force_ref[entry]
        first_ref[entry + 1] = force_ref[entry] * inverse_theta

    def edges(ref):
        ref[0] = jnp.where(lower, none, pltpu.roll(ref[length], planes, axis=0))
        ref[length + 1] = jnp.where(lower, pltpu.roll(ref[1], planes, axis=0), none)

    edges(first_ref)
    correction = [first_ref[own_lead + row + 1] for row in range(rows)]
    for step in range(CHEB - 1):
        old_ref, new_ref = (first_ref, second_ref) if step % 2 == 0 else (second_ref, first_ref)
        keep = table_ref[TABLE_AT["keep", step]]
        gain = table_ref[TABLE_AT["gain", step]]
        for entry in range(length):
            value = old_ref[entry + 1]
            flow = coef_ref[6, entry] * value - coef_ref[0, entry] * old_ref[entry]
            flow = flow - coef_ref[1, entry] * old_ref[entry + 2]
            side = coef_ref[2, entry] * pltpu.roll(value, 1, axis=1)
            side = side + coef_ref[3, entry] * pltpu.roll(value, 127, axis=1)
            deep = coef_ref[4, entry] * pltpu.roll(value, 1, axis=0)
            deep = deep + coef_ref[5, entry] * pltpu.roll(value, 7, axis=0)
            mismatch = mismatch_ref[entry] - (flow - (side + deep))
            if step < CHEB - 2:
                mismatch_ref[entry] = mismatch
            new_ref[entry + 1] = keep * value + gain * mismatch
        if step < CHEB - 2:
            edges(new_ref)
        correction = [held + new_ref[own_lead + row + 1] for row, held in enumerate(correction)]

    def cut(value):
        value = jnp.where(own_upper, pltpu.roll(value, planes, axis=0), value)
        return pltpu.roll(value, 128 - margin, axis=1)[0:planes, 0:tile]

    for row in range(rows):
        entry = own_lead + row
        found = cut(base_ref[entry + REACH] + force_ref[entry] + correction[row])
        for at in range(planes):
            temperature_ref[at, row : row + 1, :] = found[at : at + 1]

    upper = jnp.where(own_upper, 1, 0)
    raw = jnp.where(lower, 0, 1) == upper
    middle = (lane >= margin) & (lane < margin + tile)
    cells = Packed(own_lead, upper, planes, raw, middle, far_ref, near_ref, code_ref)
    for axis, found in enumerate(flux_of(cells, table)):
        for row in range(2):
            turned = pltpu.roll(found, 128 - margin - row * tile, axis=1)[:, 0:tile]
            for half in range(2):
                for at in range(planes):
                    line, place = half * planes + at, row + 2 * half
                    flux_ref[axis, at, place : place + 1, :] = turned[line : line + 1]


def on_device(
    thermal_deviation_iterate,
    volumetric_source_term,
    node_substance_label,
    spectral_table_lookup,
    propagation_velocity_table,
    specific_heat_table,
    collision_frequency_table,
    ordinate_inclination,
    ordinate_longitude,
):
    planes, rows, width = thermal_deviation_iterate.shape
    modes, space = lax.axis_size("modes"), lax.axis_size("space")
    tile = width // modes
    per_part = spectral_table_lookup.shape[0]
    half_dir = ordinate_inclination.shape[0]
    assert planes == 4 and rows == 4 and width == 256
    assert modes == 4 and per_part <= PART and half_dir <= PART
    halo = -(-REACH_COLUMNS // rows)
    assert tile * 2 == 128 and 3 * rows * planes // 8 * REACH_COLUMNS + per_part <= 128
    vmem = pl.BlockSpec(memory_space=pltpu.VMEM)
    parts = rows * planes // 8
    depth = 3 * parts + 1
    arguments = (
        thermal_deviation_iterate,
        volumetric_source_term,
        node_substance_label,
        spectral_table_lookup,
        propagation_velocity_table,
        specific_heat_table,
        collision_frequency_table.T,
        ordinate_inclination,
        ordinate_longitude,
    )
    held = [(pltpu.SMEM if at == 3 else pltpu.VMEM)(x.shape, x.dtype) for at, x in enumerate(arguments)]
    part_shape = pltpu.VMEM((depth, 8, 128), jnp.float32)
    payload, crossing, small = pl.pallas_call(
        pack_kernel,
        out_shape=(part_shape, part_shape, pltpu.VMEM((16, 128), jnp.float32)),
        in_specs=[pl.BlockSpec(memory_space=pltpu.HBM)] * len(arguments),
        out_specs=(vmem, vmem, vmem),
        scratch_shapes=held + [pltpu.VMEM((depth - 1, 8, width), jnp.float32), pltpu.SemaphoreType.DMA((len(arguments),))],
        name="pack",
    )(*arguments)

    if space == 8:
        groups = 4
        fetched = []
        for apart, across in zip((*zip(*APART), (APART_BOTH,) * 2), ACROSS):
            moves = []
            for m in range(modes):
                for s in range(space):
                    source = s ^ apart[m % 2]
                    if abs(source - s) > halo:
                        source = s
                    moves.append(((m ^ across) * space + source, m * space + s))
            fetched.append(lax.ppermute(crossing if across >= 2 else payload, ("modes", "space"), moves))
        swapped = [lax.ppermute(block, "modes", [(m, m ^ 1) for m in range(modes)]) for block in fetched[:3]]
        blocks = [payload] + fetched + swapped
        lookups, masks = fetched[:3], (0,) + ACROSS[:3]

        def places():
            m, s = lax.axis_index("modes"), lax.axis_index("space")
            held = [(0,) + APART[c] + (APART_BOTH,) + APART[1 - c] for c in range(2)]
            leads, holders = [], []
            for step in range(groups):
                leads.append(lax.rem(s ^ step, groups) * rows)
                holders.append([[held[c].index(apart) for c in range(2)] for apart in (step, step ^ groups)])
            return leads, s >= groups, holders, lax.rem(m, 2) == 0, lax.rem(s, groups) * rows, s >= groups

    else:
        groups = halo + 1
        everything = lax.all_gather(payload, "space", axis=0, tiled=False)
        everything = jnp.pad(everything, ((halo, halo + 1), (0, 0), (0, 0), (0, 0)))
        first = lax.axis_index("space")
        near = lax.dynamic_slice_in_dim(everything, first, 2 * groups, 0)
        blocks = [near[at] for at in range(2 * groups)]
        lookups, masks = [], tuple(range(modes))
        for apart in range(1, modes):
            lookups.append(lax.ppermute(payload, "modes", [(m, m ^ apart) for m in range(modes)]))

        def places():
            holders = [[[step] * 2, [step + groups] * 2] for step in range(groups)]
            return [step * rows for step in range(groups)], False, holders, True, halo * rows, False

    tables = pl.pallas_call(
        lambda *refs: table_kernel(masks, per_part, half_dir, *refs),
        out_shape=pltpu.VMEM((len(TABLES), 8, 128), jnp.float32),
        in_specs=[vmem] * (len(lookups) + 1),
        out_specs=vmem,
        compiler_params=pltpu.CompilerParams(vmem_limit_bytes=8 * 1024 * 1024),
        scratch_shapes=[
            pltpu.VMEM((8 * len(GROUPS), 128), jnp.float32),
            pltpu.VMEM((128 * COLUMN_TILES, 128), jnp.float32),
        ],
        name="tables",
    )(
        *lookups,
        small,
    )
    length = groups * rows
    whole = length + 2 * REACH
    return pl.pallas_call(
        lambda *refs: main_kernel(groups, places, *refs),
        out_shape=(
            jax.ShapeDtypeStruct((planes, rows, tile), jnp.float32),
            jax.ShapeDtypeStruct((3, planes, rows, tile), jnp.float32),
        ),
        in_specs=[vmem] * (2 * groups + 1),
        out_specs=(vmem, vmem),
        scratch_shapes=[
            pltpu.VMEM((whole, 8, 128), jnp.float32),
            pltpu.VMEM((whole, 8, 128), jnp.float32),
            pltpu.VMEM((whole, 8, 128), jnp.int32),
            pltpu.VMEM((len(FAR), whole, 8, 128), jnp.float32),
            pltpu.VMEM((len(NEAR), whole, 8, 128), jnp.float32),
            pltpu.VMEM((len(NEAR), whole, 8, 128), jnp.int32),
            pltpu.VMEM((whole, 8, 128), jnp.float32),
            pltpu.VMEM((length, 8, 128), jnp.float32),
            pltpu.VMEM((7, length, 8, 128), jnp.float32),
            pltpu.VMEM((length, 8, 128), jnp.float32),
            pltpu.VMEM((length + 2, 8, 128), jnp.float32),
            pltpu.VMEM((length + 2, 8, 128), jnp.float32),
        ],
        compiler_params=pltpu.CompilerParams(vmem_limit_bytes=32 * 1024 * 1024),
        name="solve",
    )(*blocks, tables)


def solution(mesh):
    placed = (
        P(None, "space", None),
        P(None, "space", None),
        P(None, "space", None),
        P("modes"),
        P(),
        P(),
        P(),
        P(),
        P(),
    )
    return jax.shard_map(
        on_device,
        mesh=mesh,
        in_specs=placed,
        out_specs=(P(None, "space", "modes"), P(None, None, "space", "modes")),
        check_vma=False,
    )
```

```python
import itertools

import jax
import jax.numpy as jnp
from jax import lax
from jax.experimental import pallas as pl
from jax.experimental.pallas import tpu as pltpu
from jax.sharding import PartitionSpec as P


SWEEPS = 3
CHEB = 16
REACH_COLUMNS = SWEEPS + CHEB - 1
PART = 32
CODES = (0, 1, 3)
HIGHEST = lax.Precision.HIGHEST
APART = ((6, 2, 5), (7, 1, 4))
APART_BOTH = 3
ACROSS = (2, 3, 1, 0)


def monomials(degree):
    found = []
    for axes in itertools.combinations_with_replacement(range(3), degree):
        distinct = sorted(set(axes))
        for rest in itertools.product((-1, 1), repeat=max(len(distinct) - 1, 0)):
            found.append((axes, tuple(zip(distinct, (-1,) + rest)) if distinct else ()))
    return found


MONO = {degree: monomials(degree) for degree in range(4)}


def canonical(steps):
    axes = tuple(sorted(axis for axis, _ in steps))
    signs = dict(steps)
    first = signs[axes[0]]
    pattern = tuple((axis, signs[axis] * -first) for axis in sorted(signs))
    return (axes, pattern), -first


PAIRS = {CODES[a] + CODES[b]: [(1, (a, b))] for a, b in itertools.combinations_with_replacement(range(3), 2)}
TRIPLES = {
    CODES[a] + CODES[b] + CODES[c]: [(1, (a, b, c))]
    for a, b, c in itertools.combinations_with_replacement(range(3), 3)
    if (a, b, c) not in ((1, 1, 1), (2, 2, 2))
}
SINGLES = {CODES[a]: [(1, (a,))] for a in range(3)}
ALIKE = {1: 5, 2: 7}
PAIRS_ALIKE = dict(PAIRS)
EXTRA = {}
for label, place in ALIKE.items():
    PAIRS_ALIKE[place] = [(1, (label, label))]
    EXTRA[place] = [(-1, (label,) * 3)] + TRIPLES[(3 * CODES[label]) & 7]
GROUPS = {
    "u3": (3, False, PAIRS_ALIKE),
    "u2": (2, False, PAIRS_ALIKE),
    "u1d": (2, False, SINGLES),
    "u1": (1, False, SINGLES),
    "u0d": (1, True, SINGLES),
    "u0": (0, True, SINGLES),
    "a3": (4, False, TRIPLES),
    "x3": (4, False, EXTRA),
    "a2": (3, False, TRIPLES),
    "x2": (3, False, EXTRA),
    "v1d": (3, False, PAIRS),
    "v1": (2, False, PAIRS),
    "f0d": (2, False, SINGLES),
}
GROUP_AT = {name: at for at, name in enumerate(GROUPS)}
COLUMNS = (
    [("u", degree, mono) for degree in (3, 2, 1, 0) for mono in MONO[degree]]
    + [("v", degree, mono) for degree in (3, 2, 1) for mono in MONO[degree]]
    + [(axis, degree, mono) for axis in range(3) for degree in (3, 2, 1) for mono in MONO[degree]]
)
COLUMN_AT = {column: at for at, column in enumerate(COLUMNS)}
COLUMN_TILES = -(-len(COLUMNS) // 128)


def table_list():
    found = [("inverse_rate",), ("conduct",), ("inverse_theta",)]
    found += [("keep", step) for step in range(CHEB - 1)] + [("gain", step) for step in range(CHEB - 1)]
    for group, degree in (("u3", 3), ("u2", 2), ("u1d", 2), ("u1", 1), ("u0d", 1), ("u0", 0)):
        found += [(group, "u", degree, mono) for mono in MONO[degree]]
    for kind in ("v", 0, 1, 2):
        for group, degree in (("a3", 3), ("x3", 3), ("a2", 2), ("x2", 2), ("v1d", 2), ("v1", 1)):
            if kind == "v" and group[0] == "x":
                continue
            found += [(group, kind, degree, mono) for mono in MONO[degree]]
    for kind in (0, 1, 2):
        found += [("f0d", kind, 1, mono) for mono in MONO[1]]
    return found


TABLES = table_list()
TABLE_AT = {key: at for at, key in enumerate(TABLES)}


def lanes(shape):
    return lax.broadcasted_iota(jnp.int32, shape, len(shape) - 1)


def sublanes(shape):
    return lax.broadcasted_iota(jnp.int32, shape, len(shape) - 2)


def pack_kernel(*refs):
    inputs, (own_ref, cross_ref, small_ref), held = refs[:9], refs[9:12], refs[12:21]
    out_ref, sems = refs[21:]
    copies = [pltpu.make_async_copy(source, to, sems.at[at]) for at, (source, to) in enumerate(zip(inputs, held))]
    for copy in copies:
        copy.start()
    values_ref, source_ref, label_ref, lookup_ref, velocity_ref, heat_ref, rate_ref, polar_ref, azimuth_ref = held
    planes, rows, _ = values_ref.shape
    part = rows * planes // 8
    lane = lanes((8, 128))
    copies[3].wait()
    found = jnp.zeros((8, 128), jnp.int32)
    for at in range(lookup_ref.shape[0]):
        found = jnp.where(lane == 3 * part * REACH_COLUMNS + at, lookup_ref[at] + 1, found)
    extras = [found.astype(jnp.float32)] * 2
    for which, ref in enumerate((values_ref, source_ref, label_ref)):
        copies[which].wait()
        for plane in range(planes):
            for row in range(rows):
                at, sub = divmod(row * planes + plane, 8)
                value = ref[plane, row : row + 1, :]
                if which == 2:
                    value = (value + 1).astype(jnp.float32)
                out_ref[which * part + at, sub : sub + 1, :] = value
    left = lax.axis_index("modes") < lax.axis_size("modes") // 2
    for at in range(3 * part):
        sides = out_ref[at, :, 0:128], out_ref[at, :, 128:256]
        own_ref[at] = jnp.where(left, sides[0], sides[1])
        cross_ref[at] = jnp.where(left, sides[1], sides[0])
        place = at * REACH_COLUMNS
        here = (lane >= place) & (lane < place + REACH_COLUMNS)
        extras[0] = jnp.where(here, pltpu.roll(sides[1], place, axis=1), extras[0])
        extras[1] = jnp.where(here, pltpu.roll(sides[0], (place + REACH_COLUMNS) % 128, axis=1), extras[1])
    own_ref[3 * part] = jnp.where(left, extras[0], extras[1])
    cross_ref[3 * part] = jnp.where(left, extras[1], extras[0])
    small_ref[...] = jnp.zeros(small_ref.shape, jnp.float32)
    for copy in copies[4:]:
        copy.wait()
    size, half_dir = velocity_ref.shape[0], polar_ref.shape[0]
    small_ref[10:11, :] = found[0:1].astype(jnp.float32)
    small_ref[0, 0:size] = velocity_ref[...]
    small_ref[1, 0:size] = heat_ref[...]
    small_ref[2:5, 0:size] = rate_ref[...]
    for start in range(0, 128, PART):
        small_ref[8, start : start + half_dir] = polar_ref[...]
        small_ref[9, start : start + half_dir] = azimuth_ref[...]


def table_kernel(masks, per_part, half_dir, *refs):
    lookups = refs[:-4]
    small_ref, out_ref, work_ref, axes_ref = refs[-4:]
    parts = len(masks)
    padded = -(-per_part // 8) * 8
    lane = lanes((1, 128))

    last = lookups[0].shape[0] - 1
    rows = [small_ref[10:11, :]] + [ref[last, 0:1, :] for ref in lookups]
    modes = lax.axis_index("modes")
    found = jnp.zeros((1, 128), jnp.float32)
    owner = jnp.zeros((1, 128), jnp.int32)
    for part, row in zip(masks, rows):
        place = last * REACH_COLUMNS
        row = jnp.where((lane >= place) & (lane < place + per_part), row, 0.0)
        found = found + pltpu.roll(row, (part * PART - place) % 128, axis=1)
        owner = jnp.where(lane // PART == part, modes ^ part, owner)
    index = found.astype(jnp.int32) - 1
    valid = index >= 0
    index = jnp.broadcast_to(jnp.where(valid, index, 0), (8, 128))
    picked = jnp.take_along_axis(small_ref[0:8, :], index, axis=1, mode="promise_in_bounds")
    frequency = owner * per_part + lane % PART
    spectral = (frequency.astype(jnp.float32) + 1.0) / (parts * per_part)
    velocity = jnp.where(valid, picked[0:1], 1.0)
    capacity = jnp.where(valid, picked[1:2] * spectral, 0.0)
    rates = [jnp.where(valid, picked[2 + k : 3 + k], 1.0) for k in range(3)]

    conducts, inverses = [], []
    for k in range(3):
        rate_total = jnp.sum(capacity * rates[k], axis=1, keepdims=True)
        cond_total = jnp.sum(capacity * velocity * velocity / (3.0 * rates[k]), axis=1, keepdims=True)
        conducts.append(cond_total / rate_total)
        inverses.append(1.0 / (2 * half_dir * rate_total))
    sub = sublanes((8, 128))

    def by_label(values):
        found = jnp.zeros((8, 128), jnp.float32)
        for code, value in zip(CODES, values):
            found = jnp.where(sub == code, value, found)
        return found

    out_ref[TABLE_AT["inverse_rate",]] = by_label(inverses)
    out_ref[TABLE_AT["conduct",]] = by_label(conducts)
    top = 1.0 + 12.0 * jnp.maximum(jnp.maximum(conducts[0], conducts[1]), conducts[2])
    top = jnp.broadcast_to(top, (8, 128))
    theta = (top + 1.0) / 2.0
    delta = (top - 1.0) / 2.0
    sigma = theta / delta
    rho = 1.0 / sigma
    out_ref[TABLE_AT["inverse_theta",]] = 1.0 / theta
    for step in range(CHEB - 1):
        rho_new = 1.0 / (2.0 * sigma - rho)
        out_ref[TABLE_AT["keep", step]] = rho_new * rho
        out_ref[TABLE_AT["gain", step]] = 2.0 * rho_new / delta
        rho = rho_new

    angles = small_ref[8:16, :]
    cosines, sines = jnp.cos(angles), jnp.sin(angles)
    real = (lane % PART) < half_dir
    u = [cosines[0:1], sines[0:1] * cosines[1:2], sines[0:1] * sines[1:2]]
    u = [jnp.where(real, part, 0.0) for part in u]
    a = [jnp.abs(part) for part in u]
    total = a[0] + a[1] + a[2]
    sides = [jnp.where(part >= 0.0, 1.0, -1.0) for part in u]

    products = {(): jnp.where(real, 1.0, 0.0)}
    for degree in (1, 2, 3):
        for axes in itertools.combinations_with_replacement(range(3), degree):
            products[axes] = products[axes[:-1]] * a[axes[-1]]
    masks = {}
    for degree in range(4):
        for _, pattern in MONO[degree]:
            if pattern not in masks:
                same = flipped = jnp.ones((1, 128), jnp.float32)
                for axis, sign in pattern:
                    if axis == 0:
                        flipped = jnp.zeros((1, 128), jnp.float32)
                    else:
                        same = same * jnp.where(sides[axis] == -sign, 1.0, 0.0)
                        flipped = flipped * jnp.where(sides[axis] == sign, 1.0, 0.0)
                masks[pattern] = (same + flipped, same - flipped)
    axes_ref[...] = jnp.zeros(axes_ref.shape, jnp.float32)
    weights = {"u": None, "v": total}
    weights.update({axis: u[axis] * (1.0 / (2 * half_dir)) for axis in range(3)})
    for at, (kind, degree, (axes, pattern)) in enumerate(COLUMNS):
        even, odd = masks[pattern]
        row = products[axes] * (even if kind in ("u", "v") else odd)
        if weights[kind] is not None:
            row = row * weights[kind]
        axes_ref[at : at + 1, :] = row

    columns = jnp.concatenate([velocity, capacity] + rates + [jnp.zeros((3, 128), jnp.float32)], axis=0).T

    def spread(at):
        found = jnp.zeros((padded, 128), jnp.float32)
        where = lanes((padded, 128)) // PART
        for part in range(parts):
            column = columns[part * PART : part * PART + padded, at : at + 1]
            found = jnp.where(where == part, column, found)
        return found

    speed, stored = spread(0), spread(1)
    loss = [spread(2 + k) for k in range(3)]
    inverse = [1.0 / (speed * total + loss[k]) for k in range(3)]
    weight = [stored]
    for _ in range(4):
        weight.append(weight[-1] * speed)
    chains = {}
    for length in (1, 2, 3):
        for labels in itertools.combinations_with_replacement(range(3), length):
            chains[labels] = inverse[labels[0]] if length == 1 else chains[labels[:-1]] * inverse[labels[-1]]
    work_ref[...] = jnp.zeros(work_ref.shape, jnp.float32)
    for name, (power, rated, index) in GROUPS.items():
        for code, terms in index.items():
            field = sum(sign * chains[tuple(sorted(labels))] for sign, labels in terms) * weight[power]
            if rated:
                field = field * loss[terms[0][1][0]]
            at = GROUP_AT[name] * 8 + code
            work_ref[at : at + 1, :] = jnp.sum(field, axis=0, keepdims=True)
    sums = lax.dot_general(
        work_ref[...],
        axes_ref[...],
        (((1,), (1,)), ((), ())),
        precision=HIGHEST,
        preferred_element_type=jnp.float32,
    )
    for at, key in enumerate(TABLES):
        if len(key) == 4:
            row, column = GROUP_AT[key[0]] * 8, COLUMN_AT[key[1:]]
            values = sums[row : row + 8, column : column + 1]
            if key[0] in ("u3", "u2"):
                row, column = GROUP_AT["x" + key[0][1]] * 8, COLUMN_AT[("v",) + key[2:]]
                values = values + sums[row : row + 8, column : column + 1]
            out_ref[at] = jnp.broadcast_to(values, (8, 128))


SIGNED = [(axis, sign) for axis in range(3) for sign in (-1, 1)]


def follows(earlier, step):
    return all((step[0], -step[1]) != before for before in earlier)


def displacement(steps):
    found = [0, 0, 0]
    for axis, sign in steps:
        found[axis] += sign
    return tuple(found)


def ends_of_two():
    found = {}
    for first in SIGNED:
        for second in SIGNED:
            if follows((first,), second):
                found.setdefault(tuple(sorted((first, second))), []).append(first)
    return found


ENDS = ends_of_two()
REACH = SWEEPS
FAR = [(z, y) for z in range(-3, 4) for y in range(-3, 4) if abs(z) + abs(y) <= 3]
NEAR = [(z, y) for z in range(-2, 3) for y in range(-2, 3) if abs(z) + abs(y) <= 2]
FAR_AT = {key: at for at, key in enumerate(FAR)}
NEAR_AT = {key: at for at, key in enumerate(NEAR)}


def pick(table, index):
    return jnp.take_along_axis(table, index, axis=0, mode="promise_in_bounds")


class Cells:
    def __init__(self, entry, far_ref, source_ref, code_ref):
        self.entry = entry
        self.refs = (far_ref, source_ref, code_ref)
        self.known = {}

    def get(self, which, place):
        key = (which, place)
        if key not in self.known:
            x, y, z = place
            at = FAR_AT[z, y] if which == 0 else NEAR_AT[z, y]
            self.known[key] = self.refs[which][at, self.entry + REACH + x]
        return self.known[key]

    def code(self):
        if "alike" not in self.known:
            code = self.get(2, (0, 0, 0))
            expected = jnp.where(code == CODES[0], -1, 2 * code)
            self.known["alike"] = (expected, jnp.where(code == CODES[1], ALIKE[1], ALIKE[2]))
        return self.known["alike"]

    def rise(self, place, step):
        further = list(place)
        further[step[0]] += step[1]
        return self.get(0, tuple(further)) - self.get(0, place)


class Packed(Cells):
    def __init__(self, entry, upper, planes, raw, middle, far_ref, source_ref, code_ref):
        super().__init__(entry, far_ref, source_ref, code_ref)
        self.upper, self.planes, self.raw, self.middle = upper, planes, raw, middle

    def get(self, which, place):
        key = (which, place)
        if key not in self.known:
            x, y, z = place
            at = FAR_AT[z, y] if which == 0 else NEAR_AT[z, y]
            ref = self.refs[which]
            found = []
            for row in range(2):
                entry = self.entry + (REACH + x + row)
                straight = ref[at, entry + 2 * self.upper]
                turned = ref[at, entry + 2 * (1 - self.upper)]
                found.append(jnp.where(self.raw, straight, pltpu.roll(turned, self.planes, axis=0)))
            self.known[key] = jnp.where(self.middle, found[0], pltpu.roll(found[1], 64, axis=1))
        return self.known[key]


def alike(pair, code):
    expected, place = code
    return jnp.where(pair == expected, place, pair)


class Sums:
    def __init__(self, count=4):
        self.parts = [None] * count
        self.at = 0

    def add(self, value):
        held = self.parts[self.at]
        self.parts[self.at] = value if held is None else held + value
        self.at = (self.at + 1) % len(self.parts)

    def total(self):
        held = [part for part in self.parts if part is not None]
        while len(held) > 1:
            held = [sum(held[at + 1 : at + 2], held[at]) for at in range(0, len(held), 2)]
        return held[0]


def energy_of(cells_list, table):
    sums = [Sums() for _ in cells_list]
    here = (0, 0, 0)
    codes = [cells.get(2, here) for cells in cells_list]
    rest = table(("u0", "u", 0, MONO[0][0]))
    for cells, code, held in zip(cells_list, codes, sums):
        held.add(pick(rest, code) * cells.get(1, here))
    for step in SIGNED:
        mono, _ = canonical((step,))
        rest = table(("u0d", "u", 1, mono))
        for cells, code, held in zip(cells_list, codes, sums):
            held.add(pick(rest, code) * cells.rise(here, step))
    two = {}
    for first in SIGNED:
        place = displacement((first,))
        mono, _ = canonical((first,))
        nears = [cells.get(2, place) for cells in cells_list]
        two[first] = pairs = [near + code for near, code in zip(nears, codes)]
        one, other = table(("u1", "u", 1, mono)), table(("v1", "v", 1, mono))
        for cells, near, pair, held in zip(cells_list, nears, pairs, sums):
            held.add((pick(one, near) - pick(other, pair)) * cells.get(1, place))
        for step in SIGNED:
            if follows((first,), step):
                mono, _ = canonical((first, step))
                one, other = table(("u1d", "u", 2, mono)), table(("v1d", "v", 2, mono))
                for cells, near, pair, held in zip(cells_list, nears, pairs, sums):
                    held.add((pick(one, near) - pick(other, pair)) * cells.rise(place, step))
    for steps, firsts in ENDS.items():
        place = displacement(steps)
        index = []
        for at, cells in enumerate(cells_list):
            end = cells.get(2, place)
            mine = []
            for first in firsts:
                pair = cells.get(2, displacement((first,))) + end
                mine.append((alike(pair, cells.code()), (pair + codes[at]) & 7))
            index.append(mine)
        cases = [(None, "2", canonical(steps)[0], 2)]
        cases += [(step, "3", canonical(steps + (step,))[0], 3) for step in SIGNED if follows(steps, step)]
        for step, which, mono, degree in cases:
            one, other = table(("u" + which, "u", degree, mono)), table(("a" + which, "v", degree, mono))
            for cells, mine, held in zip(cells_list, index, sums):
                factor = None
                for pair, triple in mine:
                    term = pick(one, pair) - pick(other, triple)
                    factor = term if factor is None else factor + term
                held.add(factor * (cells.get(1, place) if step is None else cells.rise(place, step)))
    return [held.total() for held in sums]


def flux_of(cells, table):
    sums = [Sums(2) for _ in range(3)]
    here = (0, 0, 0)
    code = cells.get(2, here)

    def signed(value, side):
        return value if side > 0 else -value

    for step in SIGNED:
        mono, side = canonical((step,))
        rise = signed(cells.rise(here, step), side)
        for axis in range(3):
            sums[axis].add(pick(table(("f0d", axis, 1, mono)), code) * rise)
    for first in SIGNED:
        place = displacement((first,))
        pair = cells.get(2, place) + code
        mono, side = canonical((first,))
        value = signed(cells.get(1, place), side)
        for axis in range(3):
            sums[axis].add(pick(table(("v1", axis, 1, mono)), pair) * value)
        for step in SIGNED:
            if follows((first,), step):
                mono, side = canonical((first, step))
                value = signed(cells.rise(place, step), side)
                for axis in range(3):
                    sums[axis].add(pick(table(("v1d", axis, 2, mono)), pair) * value)
    for steps, firsts in ENDS.items():
        place = displacement(steps)
        end = cells.get(2, place)
        index = []
        for first in firsts:
            pair = cells.get(2, displacement((first,))) + end
            index.append((alike(pair, cells.code()), (pair + code) & 7))
        cases = [(None, "2", canonical(steps), 2)]
        cases += [(step, "3", canonical(steps + (step,)), 3) for step in SIGNED if follows(steps, step)]
        for step, which, (mono, side), degree in cases:
            value = signed(cells.get(1, place) if step is None else cells.rise(place, step), side)
            for axis in range(3):
                one, other = table(("a" + which, axis, degree, mono)), table(("x" + which, axis, degree, mono))
                factor = None
                for pair, triple in index:
                    term = pick(one, triple) - pick(other, pair)
                    factor = term if factor is None else factor + term
                sums[axis].add(factor * value)
    return [held.total() for held in sums]


def shift_plane(value, z, planes):
    if z == 0:
        return value
    plane = sublanes((8, 128)) % planes
    return jnp.where((plane + z >= 0) & (plane + z < planes), pltpu.roll(value, (-z) % 8, axis=0), 0.0)


def place_groups(pairs, leads, swap, rows, planes, fields):
    parts = rows * planes // 8
    lane, lower = lanes((8, 128)), sublanes((8, 128)) < planes
    modes = lax.axis_index("modes")
    odd, chip = lax.rem(modes, 2), modes // 2
    start = jnp.where(odd == 1, 0, 128 - REACH_COLUMNS)
    zone = (lane >= start) & (lane < start + REACH_COLUMNS)
    beyond = zone & (lane * 0 + odd + chip != 1)

    for both, lead in zip(pairs, leads):

        def halves(at):
            first, second = both(at)
            low, high = jnp.where(swap, second, first), jnp.where(swap, first, second)
            return (
                jnp.where(lower, low, pltpu.roll(high, planes, axis=0)),
                jnp.where(lower, pltpu.roll(low, planes, axis=0), high),
            )

        extras = halves(3 * parts)
        for which, ref in enumerate(fields):
            for part in range(parts):
                place = which * parts + part
                for row, (main, extra) in enumerate(zip(halves(place), extras)):
                    extra = pltpu.roll(extra, lax.rem(start - place * REACH_COLUMNS + 128, 128), axis=1)
                    value = jnp.where(beyond, 0.0, jnp.where(zone, extra, main))
                    ref[REACH + lead + 2 * part + row] = value.astype(ref.dtype)


def pairs_of(blocks, holders):
    core_first = lax.rem(lax.axis_index("modes"), 2) == 0

    def block(holder, at):
        first, second = [blocks[held] for held in holder]
        return first[at] if first is second else jnp.where(core_first, first[at], second[at])

    return [lambda at, pair=pair: [block(holder, at) for holder in pair] for pair in holders]


def main_kernel(places, holders, length, *refs):
    count = 2 * len(holders)
    blocks = refs[:count]
    table_ref, temperature_ref, flux_ref = refs[count : count + 3]
    far_ref, near_ref, code_ref, label_ref, base_ref, source_base_ref = refs[count + 3 : count + 9]
    kappa_ref, force_ref, coef_ref, mismatch_ref, first_ref, second_ref = refs[count + 9 :]
    planes, rows, tile = temperature_ref.shape
    lane, sub = lanes((8, 128)), sublanes((8, 128))
    lower = sub < planes
    plane = sub % planes
    leads, swap, own_lead, own_upper = places()
    fields = base_ref, source_base_ref, label_ref
    place_groups(pairs_of(blocks, holders), leads, swap, rows, planes, fields)

    for at in range(REACH, REACH + length):
        label = label_ref[at]
        code = jnp.where(label == 3, CODES[2], jnp.maximum(label - 1, 0))
        for value, ref, keys in ((base_ref[at], far_ref, FAR), (source_base_ref[at], near_ref, NEAR), (code, code_ref, NEAR)):
            for y in sorted({y for _, y in keys}):
                moved = pltpu.roll(value, (-y) % 128, axis=1) if y else value
                for index, (z, other) in enumerate(keys):
                    if other == y and ref is not code_ref:
                        ref[index, at] = shift_plane(moved, z, planes)
                    elif other == y:
                        ref[index, at] = pltpu.roll(moved, (-z) % 8, axis=0) if z else moved

    for ref, keys, reach in ((far_ref, FAR, 3), (near_ref, NEAR, 2), (code_ref, NEAR, 2), (label_ref, None, 1)):
        none = jnp.zeros((8, 128), ref.dtype)
        for index, (z, y) in enumerate(keys or [(0, 0)]):
            for at in range(REACH):
                for entry, other, low in ((at, at + length, False), (length + REACH + at, REACH + at, True)):
                    beyond = at + 1 if low else REACH - at
                    if abs(z) + abs(y) + beyond <= reach:
                        value = ref[index, other] if keys else ref[other]
                        value = pltpu.roll(value, planes, axis=0)
                        value = jnp.where(lower, value, none) if low else jnp.where(lower, none, value)
                        if keys:
                            ref[index, entry] = value
                        else:
                            ref[entry] = value

    conduct = table_ref[TABLE_AT["conduct",]]
    for at in range(REACH - 1, length + REACH + 1):
        kappa_ref[at] = jnp.where(label_ref[at] > 0, pick(conduct, code_ref[NEAR_AT[0, 0], at]), 0.0)

    def table(key):
        return table_ref[TABLE_AT[key]]

    def forcing(step, _):
        entries = (2 * step, 2 * step + 1)
        cells_list = [Cells(entry, far_ref, near_ref, code_ref) for entry in entries]
        energies = energy_of(cells_list, table)
        scale = table_ref[TABLE_AT["inverse_rate",]]
        for entry, cells, energy in zip(entries, cells_list, energies):
            force = energy * pick(scale, cells.get(2, (0, 0, 0)))
            force_ref[entry] = jnp.where(label_ref[entry + REACH] > 0, force, 0.0)
        return 0

    lax.fori_loop(0, length // 2, forcing, 0)

    none = jnp.zeros((8, 128), jnp.float32)
    inverse_theta = table_ref[TABLE_AT["inverse_theta",]]
    for entry in range(length):
        kappa = kappa_ref[entry + REACH]
        real = label_ref[entry + REACH] > 0
        others = [
            kappa_ref[entry + REACH - 1],
            kappa_ref[entry + REACH + 1],
            pltpu.roll(kappa, 1, axis=1),
            pltpu.roll(kappa, 127, axis=1),
            shift_plane(kappa, -1, planes),
            shift_plane(kappa, 1, planes),
        ]
        faces = [jnp.where(real, 0.5 * (kappa + other), 0.0) for other in others]
        coef_ref[6, entry] = 1.0 + ((faces[0] + faces[1]) + (faces[2] + faces[3]) + (faces[4] + faces[5]))
        faces[4] = jnp.where(plane >= 1, faces[4], 0.0)
        faces[5] = jnp.where(plane < planes - 1, faces[5], 0.0)
        for at in range(6):
            coef_ref[at, entry] = faces[at]
        mismatch_ref[entry] = force_ref[entry]
        first_ref[entry + 1] = force_ref[entry] * inverse_theta

    def edges(ref):
        ref[0] = jnp.where(lower, none, pltpu.roll(ref[length], planes, axis=0))
        ref[length + 1] = jnp.where(lower, pltpu.roll(ref[1], planes, axis=0), none)

    edges(first_ref)
    correction = [first_ref[own_lead + row + 1] for row in range(rows)]
    for step in range(CHEB - 1):
        old_ref, new_ref = (first_ref, second_ref) if step % 2 == 0 else (second_ref, first_ref)
        keep = table_ref[TABLE_AT["keep", step]]
        gain = table_ref[TABLE_AT["gain", step]]
        for entry in range(length):
            value = old_ref[entry + 1]
            flow = coef_ref[6, entry] * value - coef_ref[0, entry] * old_ref[entry]
            flow = flow - coef_ref[1, entry] * old_ref[entry + 2]
            side = coef_ref[2, entry] * pltpu.roll(value, 1, axis=1)
            side = side + coef_ref[3, entry] * pltpu.roll(value, 127, axis=1)
            deep = coef_ref[4, entry] * pltpu.roll(value, 1, axis=0)
            deep = deep + coef_ref[5, entry] * pltpu.roll(value, 7, axis=0)
            mismatch = mismatch_ref[entry] - (flow - (side + deep))
            if step < CHEB - 2:
                mismatch_ref[entry] = mismatch
            new_ref[entry + 1] = keep * value + gain * mismatch
        if step < CHEB - 2:
            edges(new_ref)
        correction = [held + new_ref[own_lead + row + 1] for row, held in enumerate(correction)]

    odd = lax.rem(lax.axis_index("modes"), 2)

    def cut(value):
        value = jnp.where(own_upper, pltpu.roll(value, planes, axis=0), value)
        return pltpu.roll(value, odd * tile, axis=1)[0:planes, 0:tile]

    for row in range(rows):
        entry = own_lead + row
        found = cut(far_ref[FAR_AT[0, 0], entry + REACH] + force_ref[entry] + correction[row])
        for at in range(planes):
            temperature_ref[at, row : row + 1, :] = found[at : at + 1]

    upper = jnp.where(own_upper, 1, 0)
    raw = jnp.where(lower, 0, 1) == upper
    middle = lane // tile == odd
    cells = Packed(own_lead, upper, planes, raw, middle, far_ref, near_ref, code_ref)
    for axis, found in enumerate(flux_of(cells, table)):
        for row in range(2):
            turned = pltpu.roll(found, (odd if row == 0 else 1 - odd) * tile, axis=1)[:, 0:tile]
            for half in range(2):
                for at in range(planes):
                    line, place = half * planes + at, row + 2 * half
                    flux_ref[axis, at, place : place + 1, :] = turned[line : line + 1]


def on_device(
    thermal_deviation_iterate,
    volumetric_source_term,
    node_substance_label,
    spectral_table_lookup,
    propagation_velocity_table,
    specific_heat_table,
    collision_frequency_table,
    ordinate_inclination,
    ordinate_longitude,
):
    planes, rows, width = thermal_deviation_iterate.shape
    modes, space = lax.axis_size("modes"), lax.axis_size("space")
    tile = width // modes
    per_part = spectral_table_lookup.shape[0]
    half_dir = ordinate_inclination.shape[0]
    assert planes == 4 and rows == 4 and width == 256
    assert modes == 4 and per_part <= PART and half_dir <= PART
    halo = -(-REACH_COLUMNS // rows)
    assert tile * 2 == 128 and 3 * rows * planes // 8 * REACH_COLUMNS + per_part <= 128
    vmem = pl.BlockSpec(memory_space=pltpu.VMEM)
    parts = rows * planes // 8
    depth = 3 * parts + 1
    arguments = (
        thermal_deviation_iterate,
        volumetric_source_term,
        node_substance_label,
        spectral_table_lookup,
        propagation_velocity_table,
        specific_heat_table,
        collision_frequency_table.T,
        ordinate_inclination,
        ordinate_longitude,
    )
    held = [(pltpu.SMEM if at == 3 else pltpu.VMEM)(x.shape, x.dtype) for at, x in enumerate(arguments)]
    part_shape = pltpu.VMEM((depth, 8, 128), jnp.float32)
    payload, crossing, small = pl.pallas_call(
        pack_kernel,
        out_shape=(part_shape, part_shape, pltpu.VMEM((16, 128), jnp.float32)),
        in_specs=[pl.BlockSpec(memory_space=pltpu.HBM)] * len(arguments),
        out_specs=(vmem, vmem, vmem),
        scratch_shapes=held + [pltpu.VMEM((depth - 1, 8, width), jnp.float32), pltpu.SemaphoreType.DMA((len(arguments),))],
        name="pack",
    )(*arguments)

    if space == 8:
        groups = 4
        fetched = []
        for apart, across in zip((*zip(*APART), (APART_BOTH,) * 2), ACROSS):
            moves = []
            for m in range(modes):
                for s in range(space):
                    source = s ^ apart[m % 2]
                    if abs(source - s) > halo:
                        source = s
                    moves.append(((m ^ across) * space + source, m * space + s))
            fetched.append(lax.ppermute(crossing if across >= 2 else payload, ("modes", "space"), moves))
        swapped = [lax.ppermute(block, "modes", [(m, m ^ 1) for m in range(modes)]) for block in fetched[:3]]
        blocks = [payload] + fetched + swapped
        lookups, masks = fetched[:3], (0,) + ACROSS[:3]

        held = [(0,) + APART[c] + (APART_BOTH,) + APART[1 - c] for c in range(2)]
        holders = [
            [[held[c].index(apart) for c in range(2)] for apart in (step, step ^ groups)] for step in range(groups)
        ]

        def places():
            s = lax.axis_index("space")
            leads = [lax.rem(s ^ step, groups) * rows for step in range(groups)]
            return leads, s >= groups, lax.rem(s, groups) * rows, s >= groups

    else:
        groups = halo + 1
        everything = lax.all_gather(payload, "space", axis=0, tiled=False)
        everything = jnp.pad(everything, ((halo, halo + 1), (0, 0), (0, 0), (0, 0)))
        first = lax.axis_index("space")
        near = lax.dynamic_slice_in_dim(everything, first, 2 * groups, 0)
        blocks = [near[at] for at in range(2 * groups)]
        lookups, masks = [], tuple(range(modes))
        for apart in range(1, modes):
            lookups.append(lax.ppermute(payload, "modes", [(m, m ^ apart) for m in range(modes)]))

        def places():
            return [step * rows for step in range(groups)], False, halo * rows, False

        holders = [[[step] * 2, [step + groups] * 2] for step in range(groups)]

    tables = pl.pallas_call(
        lambda *refs: table_kernel(masks, per_part, half_dir, *refs),
        out_shape=pltpu.VMEM((len(TABLES), 8, 128), jnp.float32),
        in_specs=[vmem] * (len(lookups) + 1),
        out_specs=vmem,
        compiler_params=pltpu.CompilerParams(vmem_limit_bytes=8 * 1024 * 1024),
        scratch_shapes=[
            pltpu.VMEM((8 * len(GROUPS), 128), jnp.float32),
            pltpu.VMEM((128 * COLUMN_TILES, 128), jnp.float32),
        ],
        name="tables",
    )(
        *lookups,
        small,
    )
    length = groups * rows
    whole = length + 2 * REACH

    return pl.pallas_call(
        lambda *refs: main_kernel(places, holders, length, *refs),
        out_shape=(
            jax.ShapeDtypeStruct((planes, rows, tile), jnp.float32),
            jax.ShapeDtypeStruct((3, planes, rows, tile), jnp.float32),
        ),
        in_specs=[vmem] * (2 * groups + 1),
        out_specs=(vmem, vmem),
        scratch_shapes=[
            pltpu.VMEM((len(FAR), whole, 8, 128), jnp.float32),
            pltpu.VMEM((len(NEAR), whole, 8, 128), jnp.float32),
            pltpu.VMEM((len(NEAR), whole, 8, 128), jnp.int32),
            pltpu.VMEM((whole, 8, 128), jnp.int32),
            pltpu.VMEM((whole, 8, 128), jnp.float32),
            pltpu.VMEM((whole, 8, 128), jnp.float32),
            pltpu.VMEM((whole, 8, 128), jnp.float32),
            pltpu.VMEM((length, 8, 128), jnp.float32),
            pltpu.VMEM((7, length, 8, 128), jnp.float32),
            pltpu.VMEM((length, 8, 128), jnp.float32),
            pltpu.VMEM((length + 2, 8, 128), jnp.float32),
            pltpu.VMEM((length + 2, 8, 128), jnp.float32),
        ],
        compiler_params=pltpu.CompilerParams(vmem_limit_bytes=32 * 1024 * 1024),
        name="solve",
    )(*blocks, tables)


def solution(mesh):
    placed = (
        P(None, "space", None),
        P(None, "space", None),
        P(None, "space", None),
        P("modes"),
        P(),
        P(),
        P(),
        P(),
        P(),
    )
    return jax.shard_map(
        on_device,
        mesh=mesh,
        in_specs=placed,
        out_specs=(P(None, "space", "modes"), P(None, None, "space", "modes")),
        check_vma=False,
    )
```
